32 devices in a mesh: dp: 4 (over y, x), mp: 8 (over z, core).
Axes of the slice: x: 2, y: 2, z: 4, core: 2. Of those that a mesh axis runs over, the one named last changes fastest.
Arguments:
- tokens: bfloat16 [2, 4096, 2048], P(None, ('dp', 'mp')), may hold values from -6 to 6
- doc_ids: int32 [2, 4096], P(None, 'dp'), may hold values from 0 to 15, never falling along the last dimension, each value on 1 to 1024 neighbouring positions
- cotangent: bfloat16 [2, 4096, 2048], P(None, ('dp', 'mp')), may hold values from -6 to 6
- norm1_gain: bfloat16 [2048], P(('dp', 'mp')), may hold values from 0.25 to 1.75
- norm1_bias: bfloat16 [2048], P(('dp', 'mp')), may hold values from -3 to 3
- query_weight: bfloat16 [2048, 2048], P('dp', 'mp'), may hold values from -0.125 to 0.125
- query_bias: bfloat16 [16, 128], P('mp', 'dp'), may hold values from -3 to 3
- kv_weight: bfloat16 [2048, 256], P(('dp', 'mp')), may hold values from -0.125 to 0.125
- value_bias: bfloat16 [128], P(('dp', 'mp')), may hold values from -3 to 3
- out_weight: bfloat16 [2048, 2048], P('mp', 'dp'), may hold values from -1 to 1
- out_bias: bfloat16 [2048], P(('dp', 'mp')), may hold values from -3 to 3
- norm2_gain: bfloat16 [2048], P(('dp', 'mp')), may hold values from 0.25 to 1.75
- norm2_bias: bfloat16 [2048], P(('dp', 'mp')), may hold values from -3 to 3
- up_weight: bfloat16 [2048, 8192], P('dp', 'mp'), may hold values from -0.125 to 0.125
- up_bias: bfloat16 [64, 128], P('mp', 'dp'), may hold values from -3 to 3
- down_weight: bfloat16 [8192, 2048], P('mp', 'dp'), may hold values from -0.5 to 0.5
- down_bias: bfloat16 [2048], P(('dp', 'mp')), may hold values from -3 to 3
Outputs:
- output: bfloat16 [2, 4096, 2048], P(None, ('dp', 'mp'))
- input_grad: bfloat16 [2, 4096, 2048], P(None, ('dp', 'mp'))
- norm1_gain_grad: float32 [2048], P(('dp', 'mp'))
- norm1_bias_grad: float32 [2048], P(('dp', 'mp'))
- query_weight_grad: float32 [2048, 2048], P('dp', 'mp')
- query_bias_grad: float32 [16, 128], P('mp', 'dp')
- kv_weight_grad: float32 [2048, 256], P(('dp', 'mp'))
- value_bias_grad: float32 [128], P(('dp', 'mp'))
- out_weight_grad: float32 [2048, 2048], P('mp', 'dp')
- out_bias_grad: float32 [2048], P(('dp', 'mp'))
- norm2_gain_grad: float32 [2048], P(('dp', 'mp'))
- norm2_bias_grad: float32 [2048], P(('dp', 'mp'))
- up_weight_grad: float32 [2048, 8192], P('dp', 'mp')
- up_bias_grad: float32 [64, 128], P('mp', 'dp')
- down_weight_grad: float32 [8192, 2048], P('mp', 'dp')
- down_bias_grad: float32 [2048], P(('dp', 'mp'))
The draws below stay inside these ranges and needn't reach their ends.
Inputs may be any that keep to these rules, and one draw needn't show every extreme that they name: `doc_ids`: along the 4096 tokens of a micro-batch the ids never fall, so each document's tokens are consecutive; a document holds 1 to 1024 tokens.
All inputs are finite; a program needn't handle non-finite values.
Results may differ from the reference program's by a relative error of at most 0.023.
Values may be sent and summed in bfloat16 or wider, within the bound.
No kernel may reach another device: no remote copies, remote signals or barrier semaphores. Data moves between devices by JAX's collectives and lax.ppermute only.
A program may use at most 96 MiB of HBM per device.

```python
import math
import jax
import jax.numpy as jnp
import numpy as np
from jax import lax

D = 2048
H = 16
HD = 128
FF = 8192
WIN = 1024
MICRO = 2
TOKENS = 4096
N_DP = 4
N_MP = 8


def level_of(stream_key, shape, shards, smallest, largest):
    factor_of = 1.0
    for dim, shards_of in shards:
        steps = jax.random.uniform(jax.random.fold_in(jax.random.fold_in(stream_key, 6), dim), (shards_of,), jnp.float32, smallest / len(shards), largest / len(shards))
        factor_of = factor_of * jnp.repeat(jnp.exp(steps), shape[dim] // shards_of).reshape((-1,) + (1,) * (len(shape) - 1 - dim))
    return factor_of


def length_profile(number_of, total, reach, lean):
    weights = [(1 << 20) // math.isqrt(standing ** lean) + 1 for standing in range(2, number_of + 1)]
    spare, counts = total - reach - (number_of - 1), [1] * (number_of - 1)
    while spare > 0:
        free = [i for i in range(number_of - 1) if counts[i] < reach]
        pool, budget = sum([weights[i] for i in free]), spare
        for i in free:
            more = min(reach - counts[i], max(1, budget * weights[i] // pool), spare)
            counts[i] = counts[i] + more
            spare = spare - more
    return np.array([reach] + counts)


def ragged_sizes(key, amount, total, limit, skew):
    if amount == 2:
        one = jax.random.randint(key, (), max(1, total - limit), min(limit, total - 1) + 1)
        return jnp.stack([one, total - one])
    lengths = jnp.asarray(length_profile(amount, total, limit, skew), jnp.int32)
    couples = (amount - 1) // 2
    donor, sink = lengths[1:1 + 2 * couples:2], lengths[2:2 + 2 * couples:2]
    margin = jnp.minimum(donor - 1, limit - sink)
    moved = jax.random.randint(jax.random.fold_in(key, 1), (couples,), 0, 1 << 20) % (margin + 1)
    lengths = lengths.at[1:1 + 2 * couples:2].set(donor - moved).at[2:2 + 2 * couples:2].set(sink + moved)
    return lengths[jax.random.permutation(jax.random.fold_in(key, 2), amount)]


def noise(own_key, dims, deviation, reach, shards=(), kind=jnp.bfloat16):
    values = deviation * jax.random.normal(own_key, dims, jnp.float32)
    if shards:
        values = values * level_of(own_key, dims, shards, -0.22, 0.18)
    return jnp.clip(values, -reach, reach).astype(kind)


def setup_inputs(seed: int = 0) -> dict:
    streams_of = jax.random.split(jax.random.key(seed), 18)
    return {
        "tokens": noise(streams_of[0], (MICRO, TOKENS, D), 1.0, 6.0, ((1, 32),)),
        "doc_ids": jax.vmap(lambda own: jnp.searchsorted(jnp.cumsum(ragged_sizes(own, 4 * N_DP, TOKENS, WIN, 2)), jnp.arange(TOKENS), side="right"))(jax.random.split(streams_of[1], MICRO)).reshape((MICRO, TOKENS)).astype(jnp.int32),
        "cotangent": noise(streams_of[2], (MICRO, TOKENS, D), 1.0, 6.0, ((1, 32),)),
        "norm1_gain": jnp.clip(1.0 + 0.15 * jax.random.normal(streams_of[3], (D,), jnp.float32), 0.25, 1.75).astype(jnp.bfloat16),
        "norm1_bias": noise(streams_of[4], (D,), 0.5, 3.0, ((0, 32),)),
        "query_weight": noise(streams_of[5], (D, H * HD), D ** -0.5, 0.125, ((0, 4), (1, 8))),
        "query_bias": noise(streams_of[6], (H, HD), 0.5, 3.0, ((0, 8), (1, 4))),
        "kv_weight": noise(streams_of[7], (D, 2 * HD), D ** -0.5, 0.125, ((0, 32),)),
        "value_bias": noise(streams_of[8], (HD,), 0.5, 3.0, ((0, 32),)),
        "out_weight": noise(streams_of[9], (H * HD, D), (H * HD // 64) ** -0.5, 1.0, ((0, 8), (1, 4))),
        "out_bias": noise(streams_of[10], (D,), 0.5, 3.0, ((0, 32),)),
        "norm2_gain": jnp.clip(1.0 + 0.15 * jax.random.normal(streams_of[11], (D,), jnp.float32), 0.25, 1.75).astype(jnp.bfloat16),
        "norm2_bias": noise(streams_of[12], (D,), 0.5, 3.0, ((0, 32),)),
        "up_weight": noise(streams_of[13], (D, FF), D ** -0.5, 0.125, ((0, 4), (1, 8))),
        "up_bias": noise(streams_of[14], (FF // 128, 128), 0.5, 3.0, ((0, 8), (1, 4))),
        "down_weight": noise(streams_of[15], (FF, D), (FF // 64) ** -0.5, 0.5, ((0, 8), (1, 4))),
        "down_bias": noise(streams_of[16], (D,), 0.5, 3.0, ((0, 32),)),
    }


@jax.custom_vjp
def low(v):
    return lax.optimization_barrier(v.astype(jnp.bfloat16)).astype(jnp.float32)

@jax.custom_vjp
def low_back(v):
    return v

def low_keep(v):
    return (low(v), None)

def low_pass(kept, grad):
    return (grad,)

def back_keep(v):
    return (v, None)

def back_low(kept, grad):
    return (low(grad),)
low.defvjp(low_keep, low_pass)
low_back.defvjp(back_keep, back_low)
EPSILON = 1e-05
PRECISE = lax.Precision.HIGHEST

def layer_norm(tok_rows, norm_gain, norm_shift):
    row_mean = lax.optimization_barrier(jnp.mean(tok_rows, axis=-1, keepdims=True))
    centred = tok_rows - row_mean
    row_var = lax.optimization_barrier(jnp.mean(centred * centred, axis=-1, keepdims=True))
    return centred * lax.rsqrt(row_var + EPSILON) * norm_gain + norm_shift

def group_copies(tok_rows):
    return jax.vmap(low_back)(jnp.broadcast_to(tok_rows, (N_MP,) + tok_rows.shape))

def group_project(tok_rows, weight):
    copies = group_copies(tok_rows)
    width = weight.shape[1] // N_MP
    return jnp.einsum('gwd,dgc->wgc', copies, weight.reshape(weight.shape[0], N_MP, width), precision=PRECISE).reshape(tok_rows.shape[0], weight.shape[1])

def group_reduce(tok_rows, weight):
    width = weight.shape[0] // N_MP
    parts = jnp.einsum('wgc,gcd->gwd', tok_rows.reshape(tok_rows.shape[0], N_MP, width), weight.reshape(N_MP, width, weight.shape[1]), precision=PRECISE)
    return lax.optimization_barrier(jnp.sum(low(parts), axis=0))

def window_forward(params, tok_rows, doc_row):
    norm1_gain, norm1_bias, query_weight, query_bias, kv_weight, value_bias, out_weight, out_bias, norm2_gain, norm2_bias, up_weight, up_bias, down_weight, down_bias = params
    normed = low(layer_norm(tok_rows, norm1_gain, norm1_bias))
    query_rows = low_back(low(group_project(normed, query_weight) + query_bias.reshape(-1)))
    keyvalue = jnp.dot(normed, kv_weight, precision=PRECISE)
    key_rows = low_back(low(keyvalue[:, :HD]))
    value_rows = low_back(low(keyvalue[:, HD:] + value_bias))
    query_heads = query_rows.reshape(WIN, H, HD)
    block_len = min(512, WIN)
    score_scale = HD ** (-0.5)
    key_pos = jnp.arange(WIN, dtype=jnp.int32)

    def attend(block_start):
        query_block = lax.dynamic_slice_in_dim(query_heads, block_start, block_len, 0)
        query_docs = lax.dynamic_slice_in_dim(doc_row, block_start, block_len, 0)
        query_pos = block_start + jnp.arange(block_len, dtype=jnp.int32)
        allowed = (query_docs[:, None] == doc_row[None, :]) & (key_pos[None, :] <= query_pos[:, None])
        scores = low_back(jnp.einsum('qhd,kd->hqk', query_block, key_rows, precision=PRECISE) * score_scale)
        scores = jnp.where(allowed[None], scores, -1e+30)
        row_max = lax.optimization_barrier(jnp.max(scores, axis=-1, keepdims=True))
        weights = jnp.exp(scores - row_max)
        probs_low = low(weights / lax.optimization_barrier(jnp.sum(weights, axis=-1, keepdims=True)))
        return jnp.einsum('hqk,kd->qhd', probs_low, value_rows, precision=PRECISE)
    starts = jnp.arange(WIN // block_len, dtype=jnp.int32) * block_len
    context = lax.map(jax.checkpoint(attend), starts).reshape(WIN, H * HD)
    context = low_back(low(context))
    attn_out = low_back(group_reduce(context, out_weight) + out_bias)
    middle = tok_rows + attn_out
    normed_two = low(layer_norm(middle, norm2_gain, norm2_bias))
    pre_act = low_back(group_project(normed_two, up_weight) + up_bias.reshape(-1))
    hidden = low(jax.nn.gelu(pre_act, approximate=True))
    mlp_out = group_reduce(hidden, down_weight) + down_bias
    return middle + mlp_out

def reference(tokens, doc_ids, cotangent, norm1_gain, norm1_bias, query_weight, query_bias, kv_weight, value_bias, out_weight, out_bias, norm2_gain, norm2_bias, up_weight, up_bias, down_weight, down_bias):
    params = tuple((weight.astype(jnp.float32) for weight in (norm1_gain, norm1_bias, query_weight, query_bias, kv_weight, value_bias, out_weight, out_bias, norm2_gain, norm2_bias, up_weight, up_bias, down_weight, down_bias)))
    windows = tokens.astype(jnp.float32).reshape(MICRO * N_DP, WIN, D)
    doc_rows = doc_ids.reshape(MICRO * N_DP, WIN)
    cot_rows = cotangent.astype(jnp.float32).reshape(MICRO * N_DP, WIN, D)

    def one_window(totals, inputs):
        tok_rows, doc_row, cot_row = inputs
        result, pullback = jax.vjp(lambda weight_set, rows_in: window_forward(weight_set, rows_in, doc_row), params, tok_rows)
        weight_grads, row_grads = pullback(cot_row)
        totals = jax.tree.map(jnp.add, totals, weight_grads)
        return (totals, (result.astype(jnp.bfloat16), row_grads.astype(jnp.bfloat16)))
    zero_grads = tuple((jnp.zeros(weight.shape, jnp.float32) for weight in params))
    totals, (outputs, input_rows) = lax.scan(one_window, zero_grads, (windows, doc_rows, cot_rows))
    output = outputs.reshape(MICRO, N_DP * WIN, D)
    input_grad = input_rows.reshape(MICRO, N_DP * WIN, D)
    return (output, input_grad, totals[0], totals[1], totals[2], totals[3], totals[4], totals[5], totals[6], totals[7], totals[8], totals[9], totals[10], totals[11], totals[12], totals[13])
```

```python
import jax
import jax.numpy as jnp
from jax import lax
from jax.experimental import pallas as pl
from jax.experimental.pallas import tpu as pltpu
from jax.sharding import PartitionSpec as P

HD = 128
EPSILON = 1e-05
LOW = jnp.bfloat16
WIDE = jnp.float32


def norm_stats(rows):
    mean = jnp.mean(rows, axis=-1, keepdims=True)
    centred = rows - mean
    var = jnp.mean(centred * centred, axis=-1, keepdims=True)
    scale = lax.rsqrt(var + EPSILON)
    return centred * scale, scale


def norm_forward(rows, gain, shift):
    xhat, scale = norm_stats(rows)
    return xhat * gain + shift


def norm_backward(rows, gain, grad):
    xhat, scale = norm_stats(rows)
    scaled = grad * gain
    inner = (
        scaled
        - jnp.mean(scaled, axis=-1, keepdims=True)
        - xhat * jnp.mean(scaled * xhat, axis=-1, keepdims=True)
    )
    return scale * inner, jnp.sum(grad * xhat, axis=0), jnp.sum(grad, axis=0)


def gelu_pair(values):
    inner = 0.7978845608028654 * (values + 0.044715 * values * values * values)
    bent = jnp.tanh(inner)
    half = 0.5 * (1.0 + bent)
    slope = half + 0.5 * values * (1.0 - bent * bent) * 0.7978845608028654 * (
        1.0 + 3.0 * 0.044715 * values * values
    )
    return values * half, slope


def contract(left, right, left_dim, right_dim):
    return lax.dot_general(
        left, right, (((left_dim,), (right_dim,)), ((), ())), preferred_element_type=WIDE
    )


def swap_core(block):
    count = lax.axis_size("mp")
    return lax.ppermute(block, "mp", [(i, i ^ 1) for i in range(count)])


def shift_line(block, hops):
    count = lax.axis_size("mp")
    return lax.ppermute(block, "mp", [(i, (i + 2 * hops) % count) for i in range(count)])


def swap_dp(block, bit):
    count = lax.axis_size("dp")
    return lax.ppermute(block, "dp", [(i, i ^ bit) for i in range(count)])


def swap_mp(block, bit):
    count = lax.axis_size("mp")
    return lax.ppermute(block, "mp", [(i, i ^ bit) for i in range(count)])


def fence(*values):
    return lax.optimization_barrier(values)


def line_pairs(moves):
    return [(2 * source + side, 2 * target + side) for source, target in moves for side in (0, 1)]


def line_order():
    count = lax.axis_size("mp") // 2
    line = lax.axis_index("mp") // 2
    if count == 4:
        low_side = line < 2
        return [line, line ^ 1, jnp.where(low_side, 2, 1), jnp.where(low_side, 3, 0)]
    return [(line + count - step) % count for step in range(count)]


def line_near(block):
    count = lax.axis_size("mp") // 2
    if count == 4:
        return jnp.concatenate([block, swap_mp(block, 2)], axis=0)
    return jnp.concatenate([block] + [shift_line(block, i) for i in range(1, count // 2)], axis=0)


def line_across(block, near):
    count = lax.axis_size("mp") // 2
    if count == 4:
        return lax.ppermute(near, "mp", line_pairs([(1, 2), (2, 1)]))
    return jnp.concatenate([shift_line(block, i) for i in range(count // 2, count)], axis=0)


def line_out(across):
    if lax.axis_size("mp") // 2 == 4:
        line = lax.axis_index("mp") // 2
        outward = lax.ppermute(across, "mp", line_pairs([(1, 0), (2, 3)]))
        return jnp.where((line == 1) | (line == 2), across, outward)
    return across


def middle_swap(block):
    return lax.ppermute(block, "mp", line_pairs([(1, 2), (2, 1)]))


def move_out(block):
    return lax.ppermute(block, "mp", line_pairs([(1, 0), (2, 3)]))


def move_in(block):
    return lax.ppermute(block, "mp", line_pairs([(0, 1), (3, 2)]))


def plus(left, right):
    return (left.astype(WIDE) + right.astype(WIDE)).astype(LOW)


def four_places():
    return lax.axis_size("mp") // 2 == 4


def gather_1(own):
    if four_places():
        return swap_mp(own, 2), middle_swap(own)
    count = lax.axis_size("mp") // 2
    near = [own] + [shift_line(own, i) for i in range(1, count // 2)]
    far = [shift_line(own, i) for i in range(count // 2, count)]
    return jnp.concatenate(near, axis=0), jnp.concatenate(far, axis=0)


def gather_near(own, first):
    return jnp.concatenate([own, first[0]], axis=0) if four_places() else first[0]


def gather_2(first):
    return (middle_swap(first[0]), move_out(first[1])) if four_places() else first


def gather_3(first, second):
    if not four_places():
        return first[1]
    line = lax.axis_index("mp") // 2
    inner = (line == 1) | (line == 2)
    last = move_out(second[0])
    return jnp.concatenate(
        [jnp.where(inner, first[1], second[1]), jnp.where(inner, second[0], last)], axis=0
    )


def reduce_1(far):
    return move_in(far[far.shape[0] // 2 :]) if four_places() else far


def reduce_2(far, got):
    if not four_places():
        return got, got
    size = far.shape[0] // 2
    return middle_swap(plus(far[size:], got)), move_in(far[:size])


def reduce_3(near, far, got):
    if four_places():
        size = near.shape[0] // 2
        return (
            swap_mp(plus(near[size:], got[0]), 2),
            middle_swap(plus(far[:size], got[1])),
        )
    count = lax.axis_size("mp") // 2
    size = near.shape[0] * 2 // count
    blocks = [half[i * size : (i + 1) * size] for half in (near, far) for i in range(count // 2)]
    return [shift_line(blocks[hops], -hops) for hops in range(1, count)]


def reduce_end(near, got):
    total = near[: got[0].shape[0]].astype(WIDE)
    for part in got:
        total = total + part.astype(WIDE)
    return total


def sum_inward(far):
    return move_in(far) if four_places() else far


def add_inward(far, got):
    return plus(far, got) if four_places() else far


def sum_across(near, passed):
    if not four_places():
        return near, passed
    size = near.shape[0] // 2
    across = middle_swap(passed)
    return near[:size].astype(WIDE) + across[:size].astype(WIDE), plus(near[size:], across[size:])


def sum_last(first, second):
    if four_places():
        return first + swap_mp(second, 2).astype(WIDE)
    return reduce_end(first, reduce_3(first, second, None))


def dp_first(block):
    count = lax.axis_size("dp")
    if count == 4:
        return [block, swap_dp(block, 1), swap_dp(block, 2)]
    blocks = [block]
    bit = 1
    while bit < count:
        size = block.shape[0]
        got = swap_dp(jnp.concatenate(blocks, axis=0), bit)
        blocks = blocks + [got[i * size : (i + 1) * size] for i in range(bit)]
        bit = bit * 2
    return blocks


def dp_second(blocks):
    if lax.axis_size("dp") == 4:
        half = blocks[0].shape[0] // 2
        head, tail = swap_dp(blocks[1][:half], 2), swap_dp(blocks[2][half:], 1)
        return list(blocks) + [jnp.concatenate([head, tail], axis=0)]
    return list(blocks)


def dp_sum_first(blocks):
    if len(blocks) == 4:
        half = blocks[0].shape[0] // 2
        head = swap_dp(blocks[3][:half], 2).astype(WIDE)
        tail = swap_dp(blocks[3][half:], 1).astype(WIDE)
        one = jnp.concatenate(
            [(blocks[1][:half].astype(WIDE) + head).astype(LOW), blocks[1][half:]], axis=0
        )
        two = jnp.concatenate(
            [blocks[2][:half], (blocks[2][half:].astype(WIDE) + tail).astype(LOW)], axis=0
        )
        return [blocks[0], one, two]
    bit = len(blocks) // 2
    size = blocks[0].shape[0]
    while bit >= 1:
        got = swap_dp(jnp.concatenate(blocks[bit:], axis=0), bit).astype(WIDE)
        blocks = [
            (blocks[i].astype(WIDE) + got[i * size : (i + 1) * size]).astype(LOW)
            for i in range(bit)
        ]
        bit = bit // 2
    return blocks


def dp_sum_second(blocks):
    total = blocks[0].astype(WIDE)
    for bit, block in enumerate(blocks[1:]):
        total = total + swap_dp(block, bit + 1).astype(WIDE)
    return total


def pack_reduce(parts):
    place = lax.axis_index("mp")
    bit = parts.shape[0] // 2
    while bit >= 1:
        parts = parts[:bit] + swap_dp(parts[bit:], bit)
        bit = bit // 2
    parts = parts[0]
    bit = parts.shape[0] // 2
    while bit >= 1:
        upper = (place & bit) != 0
        low_half, high_half = parts[:bit], parts[bit:]
        sent = swap_mp(jnp.where(upper, low_half, high_half), bit)
        parts = jnp.where(upper, high_half, low_half) + sent
        bit = bit // 2
    return parts[0]


def relative(array, axis):
    count = lax.axis_size("dp")
    place = lax.axis_index("dp")
    size = array.shape[axis] // count
    return jnp.concatenate(
        [
            lax.dynamic_slice_in_dim(array, (place ^ step) * size, size, axis)
            for step in range(count)
        ],
        axis=axis,
    )


def held(array):
    zeros = (0,) * array.ndim
    return pl.BlockSpec(array.shape, lambda *_: zeros, pipeline_mode=pl.Buffered(1))


def shaped(shape, dtype=LOW):
    return jax.ShapeDtypeStruct(shape, dtype)


def attend_kernel(n, cells, *refs):
    (own, other), refs = refs[:2], refs[2:]
    weights, refs = refs[:n], refs[n:]
    shift, keyval, query_doc, query_pos, key_doc, key_pos, query, context, probs, bias = refs
    head = pl.program_id(0)
    heads, rows, _ = query.shape
    places, size = cells

    @pl.when(head == 0)
    def _():
        allowed = (query_doc[...] == key_doc[...]) & (key_pos[...] <= query_pos[...])
        bias[...] = jnp.where(allowed, 0.0, -1e30)
        chip = jnp.concatenate([own[...], other[...]], axis=0)
        cols = weights[0].shape[1]
        for place in range(places):
            total = None
            for block in range(n):
                term = contract(
                    chip[:, block * size : (block + 1) * size],
                    weights[block][place * size : (place + 1) * size, :],
                    1,
                    0,
                )
                total = term if total is None else total + term
            total = (total + shift[:, place * cols : (place + 1) * cols]).astype(LOW)
            for i in range(cols // HD):
                query[place * (cols // HD) + i] = total[:, i * HD : (i + 1) * HD]

    scores = contract(query[head], keyval[:, :HD], 1, 1) * HD ** (-0.5) + bias[...]
    weight = jnp.exp(scores - jnp.max(scores, axis=-1, keepdims=True))
    share = 1.0 / jnp.sum(weight, axis=-1, keepdims=True)
    low = (weight * share).astype(LOW)
    probs[0] = low
    context[...] = contract(low, keyval[:, HD:], 1, 0).astype(LOW)


def attend(own, other, weights, shift, keyval, query_doc, query_pos, key_doc, key_pos):
    rows, width = own.shape
    rows = 2 * rows
    keys = keyval.shape[0]
    n = len(weights)
    size = width // n
    places = weights[0].shape[0] // size
    heads = places * weights[0].shape[1] // HD
    operands = [own, other, *weights, shift[None], keyval]
    operands += [query_doc[:, None], query_pos[:, None], key_doc[None], key_pos[None]]
    return pl.pallas_call(
        lambda *refs: attend_kernel(n, (places, size), *refs),
        grid=(heads,),
        in_specs=[held(o) for o in operands],
        out_specs=[
            pl.BlockSpec((heads, rows, HD), lambda h: (0, 0, 0)),
            pl.BlockSpec((rows, HD), lambda h: (0, h)),
            pl.BlockSpec((1, rows, keys), lambda h: (h, 0, 0)),
        ],
        out_shape=[
            shaped((heads, rows, HD)),
            shaped((rows, heads * HD)),
            shaped((heads, rows, keys)),
        ],
        scratch_shapes=[pltpu.VMEM((rows, keys), WIDE)],
        compiler_params=pltpu.CompilerParams(vmem_limit_bytes=18 * 2**20),
        cost_estimate=pl.CostEstimate(
            flops=4 * rows * keys * heads * HD + 2 * rows * width * heads * HD,
            bytes_accessed=2 * heads * rows * keys + 2 * width * heads * HD,
            transcendentals=heads * rows * keys,
        ),
    )(*operands)


def project_kernel(n, *refs):
    context, weights, (own, other) = refs[0], refs[1 : 1 + n], refs[1 + n :]
    rows = own.shape[0]
    size = weights[0].shape[1]
    for block in range(n):
        cols = slice(block * size, (block + 1) * size)
        got = contract(context[...], weights[block][...], 1, 0)
        own[:, cols] = got[:rows]
        other[:, cols] = got[rows:].astype(LOW)


def project(context, weights):
    n = len(weights)
    rows, depth = context.shape
    width = n * weights[0].shape[1]
    return pl.pallas_call(
        lambda *refs: project_kernel(n, *refs),
        out_shape=[shaped((rows // 2, width), WIDE), shaped((rows // 2, width))],
        compiler_params=pltpu.CompilerParams(vmem_limit_bytes=20 * 2**20),
        cost_estimate=pl.CostEstimate(
            flops=2 * rows * depth * width, bytes_accessed=2 * depth * width, transcendentals=0
        ),
    )(context, *weights)


def attend_back_kernel(n, heads, cells, *refs):
    (own, other), refs = refs[:2], refs[2:]
    out_weights, refs = refs[:n], refs[n:]
    query_weights, refs = refs[:n], refs[n:]
    query, keyval, probs, refs = refs[0], refs[1], refs[2], refs[3:]
    query_grad, keyval_grad, back_own, back_other, context_grad, all_grad, total = refs
    head = pl.program_id(0)
    scale = HD ** (-0.5)
    places, size = cells

    @pl.when(head == 0)
    def _():
        total[...] = jnp.zeros_like(total)
        chip = jnp.concatenate([own[...], other[...]], axis=0)
        got = None
        for block in range(n):
            term = contract(chip[:, block * size : (block + 1) * size], out_weights[block][...], 1, 1)
            got = term if got is None else got + term
        got = got.astype(LOW)
        for i in range(heads):
            context_grad[i] = got[:, i * HD : (i + 1) * HD]

    low = probs[0]
    wide = low.astype(WIDE)
    given = contract(context_grad[head], keyval[:, HD:], 1, 1)
    middle = jnp.sum(wide * given, axis=-1, keepdims=True)
    score_grad = (wide * (given - middle)).astype(LOW)
    moved = (contract(score_grad, keyval[:, :HD], 1, 0) * scale).astype(LOW)
    query_grad[...] = moved
    all_grad[head] = moved
    total[:, :HD] += contract(score_grad, query[head], 0, 0)
    total[:, HD:] += contract(low, context_grad[head], 0, 0)

    @pl.when(head == heads - 1)
    def _():
        keyval_grad[:, :HD] = (total[:, :HD] * scale).astype(LOW)
        keyval_grad[:, HD:] = total[:, HD:].astype(LOW)
        cols = query_weights[0].shape[1]
        each = cols // HD
        parts = [
            jnp.concatenate([all_grad[place * each + i] for i in range(each)], axis=1)
            for place in range(places)
        ]
        rows = back_own.shape[0]
        for block in range(n):
            got = None
            for place in range(places):
                term = contract(
                    parts[place], query_weights[block][place * size : (place + 1) * size, :], 1, 1
                )
                got = term if got is None else got + term
            back_own[:, block * size : (block + 1) * size] = got[:rows]
            back_other[:, block * size : (block + 1) * size] = got[rows:].astype(LOW)


def attend_back(own, other, out_weights, query_weights, query, keyval, probs):
    rows, width = own.shape
    heads, both, _ = query.shape
    keys = keyval.shape[0]
    n = len(out_weights)
    size = width // n
    places = query_weights[0].shape[0] // size
    first = [own, other, *out_weights, *query_weights, query, keyval]
    return pl.pallas_call(
        lambda *refs: attend_back_kernel(n, heads, (places, size), *refs),
        grid=(heads,),
        in_specs=[held(o) for o in first] + [pl.BlockSpec((1, both, keys), lambda h: (h, 0, 0))],
        out_specs=[
            pl.BlockSpec((both, HD), lambda h: (0, h)),
            pl.BlockSpec((keys, 2 * HD), lambda h: (0, 0)),
            pl.BlockSpec((rows, width), lambda h: (0, 0)),
            pl.BlockSpec((rows, width), lambda h: (0, 0)),
        ],
        out_shape=[
            shaped((both, heads * HD)),
            shaped((keys, 2 * HD)),
            shaped((rows, width), WIDE),
            shaped((rows, width)),
        ],
        scratch_shapes=[
            pltpu.VMEM((heads, both, HD), LOW),
            pltpu.VMEM((heads, both, HD), LOW),
            pltpu.VMEM((keys, 2 * HD), WIDE),
        ],
        compiler_params=pltpu.CompilerParams(vmem_limit_bytes=48 * 2**20),
        cost_estimate=pl.CostEstimate(
            flops=8 * both * keys * heads * HD + 4 * both * width * heads * HD,
            bytes_accessed=2 * heads * both * keys + 4 * width * heads * HD,
            transcendentals=0,
        ),
    )(*first, probs)


def mlp_kernel(n, *refs):
    rows_in, refs = refs[:2], refs[2:]
    grads_in, refs = refs[:2], refs[2:]
    ups, refs = refs[:n], refs[n:]
    downs, refs = refs[:n], refs[n:]
    shift, hidden, pre_grad, back, out, other = refs
    size = ups[0].shape[0]
    count = rows_in[0].shape[0]
    spans = [slice(i * size, (i + 1) * size) for i in range(n)]
    for side in (1, 0):
        pre = given = None
        for block, span in enumerate(spans):
            term = contract(rows_in[side][:, span], ups[block][...], 1, 0)
            pre = term if pre is None else pre + term
        for block, span in enumerate(spans):
            term = contract(grads_in[side][:, span], downs[block][...], 1, 1)
            given = term if given is None else given + term
        value, slope = gelu_pair(pre + shift[...])
        value = value.astype(LOW)
        grad = (given * slope).astype(LOW)
        hidden[side * count : (side + 1) * count] = value
        pre_grad[side * count : (side + 1) * count] = grad
        for block, span in enumerate(spans):
            got = contract(grad, ups[block][...], 1, 1).astype(LOW)
            if side == 0:
                back[:, span] = got
            else:
                other[:count, span] = got
        for block, span in enumerate(spans):
            got = contract(value, downs[block][...], 1, 0).astype(LOW)
            if side == 0:
                out[:, span] = got
            else:
                other[count:, span] = got


def mlp(rows_in, grads_in, ups, downs, shift):
    n = len(ups)
    count, width = rows_in[0].shape
    units = ups[0].shape[1]
    return pl.pallas_call(
        lambda *refs: mlp_kernel(n, *refs),
        out_shape=[shaped((2 * count, units))] * 2
        + [shaped((count, width))] * 2
        + [shaped((2 * count, width))],
        compiler_params=pltpu.CompilerParams(vmem_limit_bytes=34 * 2**20),
        cost_estimate=pl.CostEstimate(
            flops=16 * count * units * width,
            bytes_accessed=4 * units * width + 16 * count * width,
            transcendentals=2 * count * units,
        ),
    )(*rows_in, *grads_in, *ups, *downs, shift[None])


def up_grad_kernel(n, *refs):
    lefts, rights, result = refs[:n], refs[n : -1], refs[-1]
    per = n // len(rights)
    total = None
    for i, right in enumerate(rights):
        count = right.shape[0] // per
        for j in range(per):
            term = contract(lefts[i * per + j][...], right[j * count : (j + 1) * count], 0, 0)
            total = term if total is None else total + term
    result[0] = total.astype(LOW)


def up_grad_of(lefts, rights, blocks):
    count, width = lefts[0].shape
    units = rights[0].shape[1]
    size = width // blocks
    n = len(lefts)
    return pl.pallas_call(
        lambda *refs: up_grad_kernel(n, *refs),
        grid=(blocks,),
        in_specs=[pl.BlockSpec((count, size), lambda b: (0, b))] * n + [held(r) for r in rights],
        out_specs=pl.BlockSpec((1, size, units), lambda b: (b, 0, 0)),
        out_shape=shaped((blocks, size, units)),
        compiler_params=pltpu.CompilerParams(vmem_limit_bytes=44 * 2**20),
        cost_estimate=pl.CostEstimate(
            flops=2 * n * count * width * units,
            bytes_accessed=2 * (n * count * (width + units) + width * units),
            transcendentals=0,
        ),
    )(*lefts, *rights)


def down_grad_kernel(n, *refs):
    lefts, rights, result = refs[: -n - 1], refs[-n - 1 : -1], refs[-1]
    per = n // len(lefts)
    blocks, _, size = result.shape
    for block in range(blocks):
        total = None
        for i, left in enumerate(lefts):
            count = left.shape[0] // per
            for j in range(per):
                term = contract(
                    left[j * count : (j + 1) * count],
                    rights[i * per + j][:, block * size : (block + 1) * size],
                    0,
                    0,
                )
                total = term if total is None else total + term
        result[block] = total.astype(LOW)


def down_grad_of(lefts, rights, blocks):
    count, width = rights[0].shape
    rows, units = lefts[0].shape
    n = len(rights)
    tile = min(256, units)
    return pl.pallas_call(
        lambda *refs: down_grad_kernel(n, *refs),
        grid=(units // tile,),
        in_specs=[pl.BlockSpec((rows, tile), lambda u: (0, u))] * len(lefts)
        + [held(r) for r in rights],
        out_specs=pl.BlockSpec((blocks, tile, width // blocks), lambda u: (0, u, 0)),
        out_shape=shaped((blocks, units, width // blocks)),
        compiler_params=pltpu.CompilerParams(vmem_limit_bytes=44 * 2**20),
        cost_estimate=pl.CostEstimate(
            flops=2 * n * count * width * units,
            bytes_accessed=2 * (n * count * (width + units) + width * units),
            transcendentals=0,
        ),
    )(*lefts, *rights)


def on_device(
    tokens,
    doc_ids,
    cotangent,
    norm1_gain,
    norm1_bias,
    query_weight,
    query_bias,
    kv_weight,
    value_bias,
    out_weight,
    out_bias,
    norm2_gain,
    norm2_bias,
    up_weight,
    up_bias,
    down_weight,
    down_bias,
):
    n_dp, n_mp = lax.axis_size("dp"), lax.axis_size("mp")
    n_line = n_mp // 2
    dp, mp = lax.axis_index("dp"), lax.axis_index("mp")
    line, core = mp // 2, mp % 2
    micro, rows, width = tokens.shape
    window = doc_ids.shape[1]
    part = norm1_gain.shape[0]
    kv_part = kv_weight.shape[0]
    heads_part = query_bias.shape[0]
    units_part = up_bias.shape[0]
    slim = query_bias.shape[1]

    flat = micro * rows
    lanes = 2 * HD
    order = line_order()
    tok_low = relative(tokens, 2)
    cot_low = relative(cotangent, 2)
    vectors = [norm1_gain, norm1_bias, out_bias, norm2_gain, norm2_bias, down_bias]
    vectors += [value_bias, query_bias.reshape(-1), up_bias.reshape(-1)]
    table = jnp.stack([jnp.pad(v, (0, lanes - v.shape[0])) for v in vectors])
    table = jnp.pad(table, ((0, 16 - len(vectors)), (0, 0)))
    pack = lax.all_gather(
        jnp.concatenate([kv_weight, table], axis=0), ("dp", "mp"), axis=0, tiled=True
    )

    def back_sum(got, swapped):
        return plus(got[2], swapped[: got[2].shape[0]])

    def out_sum_of(got, swapped):
        return plus(got[3], swapped[got[3].shape[0] :])

    query_near = line_near(query_weight)
    out_near = line_near(out_weight)
    up_first = dp_first(up_weight)
    query_near, out_near, cot_low, tok_low = fence(query_near, out_near, cot_low, tok_low)
    query_across = line_across(query_weight, query_near)
    cot_near = [line_near(cot_low[0])]
    query_across, out_near, cot_near, up_first = fence(query_across, out_near, cot_near, up_first)
    query_far = line_out(query_across)
    out_across = line_across(out_weight, out_near)
    up_blocks = dp_second(up_first)
    query_far, out_across, cot_near, up_blocks = fence(query_far, out_across, cot_near, up_blocks)
    query_first = dp_first(jnp.concatenate([query_near, query_far], axis=0))
    out_far = line_out(out_across)
    cot_across = [line_across(cot_low[0], cot_near[0])]
    cot_near.append(line_near(cot_low[1]))
    (pack,) = fence(pack)
    pack = pack.reshape(n_dp, n_mp, kv_part + 16, lanes)
    kv_full = relative(pack[:, :, :kv_part], 0).reshape(width, lanes)
    fixed = pack[:, :, kv_part:].astype(WIDE)
    small = relative(fixed, 0)
    gain_one, shift_one, out_shift, gain_two, shift_two, down_shift = (
        small[:, :, i, :part].reshape(width) for i in range(6)
    )
    tok_rows = [tok_low[m].astype(WIDE) for m in range(micro)]
    normed = jnp.stack([norm_forward(r, gain_one, shift_one).astype(LOW) for r in tok_rows])
    normed_other = swap_core(normed)
    query_first, out_far, normed_other, kv_full, cot_across, fixed, cot_near = fence(
        query_first, out_far, normed_other, kv_full, cot_across, fixed, cot_near
    )
    query_blocks = dp_second(query_first)
    value_shift = fixed[:, :, 6, : value_bias.shape[0]].reshape(HD)
    kv_shift = jnp.concatenate([jnp.zeros((HD,), WIDE), value_shift])
    kv_own = (contract(normed.reshape(flat, width), kv_full, 1, 0) + kv_shift).astype(LOW)
    kv_near = line_near(kv_own)
    kv_near, out_line, fixed, cot_low = fence(
        kv_near, jnp.concatenate([out_near, out_far], axis=0), fixed, cot_low
    )
    out_first = dp_first(out_line)
    kv_across = line_across(kv_own, kv_near)
    query_table = fixed[:, :, 7, : heads_part * slim].reshape(
        n_dp, n_line, 2, heads_part, slim
    )
    query_table = lax.dynamic_index_in_dim(query_table, core, 2, keepdims=False)
    query_table = query_table.transpose(1, 2, 0, 3).reshape(n_line, heads_part * HD)
    query_shift = jnp.concatenate(
        [lax.dynamic_index_in_dim(query_table, spot, 0, keepdims=False) for spot in order]
    )
    query_blocks, kv_across, query_shift = fence(query_blocks, kv_across, query_shift)
    kv_line = jnp.concatenate([kv_near, line_out(kv_across)], axis=0)
    kv_line = kv_line.reshape(n_line, flat, lanes)
    kv_stack = jnp.stack([kv_line, swap_core(kv_line)], axis=1)
    kv_stack = kv_stack.reshape(n_line, 2, micro, rows, lanes)
    keyval = [kv_stack[:, :, m].reshape(window, lanes) for m in range(micro)]
    keyval, cot_across = fence(keyval, cot_across)
    cot_far = [line_out(cot_across[0])]
    cot_across.append(line_across(cot_low[1], cot_near[1]))
    cot_own = [swap_core(cot_near[0])]
    key_starts = [(spot * 2 + side) * rows for spot in order for side in (core, 1 - core)]
    key_pos = jnp.concatenate([s + jnp.arange(rows, dtype=jnp.int32) for s in key_starts])
    query_pos = key_pos[: 2 * rows]
    context, probs, query = [], [], []
    for m in range(micro):
        key_doc = jnp.concatenate(
            [lax.dynamic_slice_in_dim(doc_ids[m], s, rows, 0) for s in key_starts]
        )
        got = attend(
            normed[m],
            normed_other[m],
            query_blocks,
            query_shift,
            keyval[m],
            key_doc[: 2 * rows],
            query_pos,
            key_doc,
            key_pos,
        )
        query.append(got[0])
        context.append(got[1])
        probs.append(got[2])
    out_first, context, cot_own, cot_far, cot_across = fence(
        out_first, context, cot_own, cot_far, cot_across
    )
    out_blocks = dp_second(out_first)
    cot_far.append(line_out(cot_across[1]))
    out_blocks, context, down_own, fixed = fence(out_blocks, context, down_weight, fixed)
    down_first = dp_first(down_own)
    middle, normed_two = [], []
    for m in range(micro):
        mine, theirs = project(context[m], out_blocks)
        middle.append(tok_rows[m] + out_shift + mine + swap_core(theirs).astype(WIDE))
        normed_two.append(norm_forward(middle[m], gain_two, shift_two).astype(LOW))
    normed_two, fixed = fence(normed_two, fixed)
    first = [gather_1(normed_two[0])]
    up_table = lax.dynamic_index_in_dim(
        fixed[:, :, 8, : units_part * slim], mp, 1, keepdims=False
    ).reshape(n_dp, units_part, slim)
    up_shift = up_table.transpose(1, 0, 2).reshape(units_part * HD)
    first, normed_two, down_first, up_shift, cot_far = fence(
        first, normed_two, down_first, up_shift, cot_far
    )
    near_rows = [gather_near(normed_two[0], first[0])]
    near_other = [swap_core(near_rows[0])]
    second = [gather_2(first[0])]
    down_blocks = dp_second(down_first)
    near_rows, near_other, second, down_blocks, cot_far, cot_near = fence(
        near_rows, near_other, second, down_blocks, cot_far, cot_near
    )

    def feed(m, half):
        rows_in = (near_rows[m], near_other[m]) if half == 0 else (far_rows[m], far_other[m])
        grads_in = (cot_near[m], cot_own[m]) if half == 0 else (cot_far[m], cot_other[m])
        return mlp(rows_in, grads_in, up_blocks, down_blocks, up_shift)

    far_rows = [gather_3(first[0], second[0])]
    cot_other = [swap_core(cot_far[0])]
    near_got = [feed(0, 0)]
    far_rows, near_got, normed_two, cot_other = fence(far_rows, near_got, normed_two, cot_other)
    first.append(gather_1(normed_two[1]))
    far_other = [swap_core(far_rows[0])]
    near_swap = [swap_core(near_got[0][4])]
    cot_own.append(swap_core(cot_near[1]))
    far_got = [feed(0, 1)]
    first, far_got, near_swap, near_got, cot_own = fence(
        first, far_got, near_swap, near_got, cot_own
    )
    second.append(gather_2(first[1]))
    far_swap = [swap_core(far_got[0][4])]
    near_rows.append(gather_near(normed_two[1], first[1]))
    near_other.append(swap_core(near_rows[1]))
    near_back = [back_sum(near_got[0], near_swap[0])]
    near_out = [out_sum_of(near_got[0], near_swap[0])]
    second, near_rows, near_other, far_swap, near_back, near_out, cot_far = fence(
        second, near_rows, near_other, far_swap, near_back, near_out, cot_far
    )
    far_back = [back_sum(far_got[0], far_swap[0])]
    far_rows.append(gather_3(first[1], second[1]))
    got_1 = [reduce_1(far_back[0])]
    cot_other.append(swap_core(cot_far[1]))
    near_got.append(feed(1, 0))
    far_rows, got_1, near_got, far_back, cot_other, far_swap = fence(
        far_rows, got_1, near_got, far_back, cot_other, far_swap
    )
    got_2 = [reduce_2(far_back[0], got_1[0])]
    far_out = [out_sum_of(far_got[0], far_swap[0])]
    far_other.append(swap_core(far_rows[1]))
    near_swap.append(swap_core(near_got[1][4]))
    far_got.append(feed(1, 1))
    got_2, near_swap, far_got, near_got, far_out = fence(
        got_2, near_swap, far_got, near_got, far_out
    )
    got_3 = [reduce_3(near_back[0], far_back[0], got_2[0])]
    far_swap.append(swap_core(far_got[1][4]))
    near_back.append(back_sum(near_got[1], near_swap[1]))
    pre_grad = [g[1] for m in range(micro) for g in (near_got[m], far_got[m])]
    row_pieces = [
        p
        for m in range(micro)
        for p in (near_rows[m], near_other[m], far_rows[m], far_other[m])
    ]
    up_grad = up_grad_of(row_pieces, pre_grad, n_dp)
    got_3, far_swap, up_grad, near_back, near_swap = fence(
        got_3, far_swap, up_grad, near_back, near_swap
    )
    far_back.append(back_sum(far_got[1], far_swap[1]))
    got_1.append(reduce_1(far_back[1]))
    up_sum = dp_sum_first([up_grad[i] for i in range(n_dp)])
    got_3, near_swap, far_swap, up_sum = fence(got_3, near_swap, far_swap, up_sum)
    near_out.append(out_sum_of(near_got[1], near_swap[1]))
    back = [reduce_end(near_back[0], got_3[0])]
    middle_grad, middle_low, middle_other = [], [], []
    norm_two_grads = []
    query_grad, keyval_grad, backs = [], [], []

    def middle_step(m):
        moved, gain_part, shift_part = norm_backward(middle[m], gain_two, back[m])
        middle_grad.append(cot_low[m].astype(WIDE) + moved)
        middle_low.append(middle_grad[m].astype(LOW))
        norm_two_grads.append((gain_part, shift_part))
        middle_other.append(swap_core(middle_low[m]))

    def attend_step(m):
        got = attend_back(
            middle_low[m], middle_other[m], out_blocks, query_blocks, query[m], keyval[m], probs[m]
        )
        query_grad.append(got[0])
        keyval_grad.append(got[1].reshape(n_line, 2, rows, lanes))
        backs.append(list(got[2:]))

    middle_step(0)
    got_1, middle_low, middle_other, far_back, far_swap, near_out, up_sum = fence(
        got_1, middle_low, middle_other, far_back, far_swap, near_out, up_sum
    )
    got_2.append(reduce_2(far_back[1], got_1[1]))
    up_weight_grad = dp_sum_second(up_sum)
    attend_step(0)
    far_out.append(out_sum_of(far_got[1], far_swap[1]))
    hidden = [g[0] for m in range(micro) for g in (near_got[m], far_got[m])]
    got_2, query_grad, hidden, far_out = fence(got_2, query_grad, hidden, far_out)
    got_3.append(reduce_3(near_back[1], far_back[1], got_2[1]))
    backs[0][1] = swap_core(backs[0][1])
    cot_pieces = [
        p for m in range(micro) for p in (cot_near[m], cot_own[m], cot_far[m], cot_other[m])
    ]
    down_grad = down_grad_of(hidden, cot_pieces, n_dp)
    got_3, down_grad, backs, up_weight_grad, far_out = fence(
        got_3, down_grad, backs, up_weight_grad, far_out
    )
    down_sum = dp_sum_first([down_grad[i] for i in range(n_dp)])
    out_inward = [sum_inward(far_out[0])]
    back.append(reduce_end(near_back[1], got_3[1]))
    middle_step(1)
    middle_low, middle_other = fence(middle_low, middle_other)

    def over_micro(left, right):
        total = contract(left[0], right[0], 0, 0)
        for m in range(1, len(left)):
            total = total + contract(left[m], right[m], 0, 0)
        return total.astype(LOW)

    out_grad = over_micro(
        context, [jnp.concatenate([middle_low[m], middle_other[m]], axis=0) for m in range(micro)]
    )
    out_grad, down_sum, far_out = fence(out_grad, down_sum, far_out)
    middle_low[1] = fence(middle_low[1], out_grad)[0]
    out_size = out_weight.shape[1]
    out_sum = dp_sum_first([out_grad[:, i * out_size : (i + 1) * out_size] for i in range(n_dp)])
    out_inward.append(sum_inward(far_out[1]))
    attend_step(1)
    query_grad, keyval_grad, out_sum, backs = fence(query_grad, keyval_grad, out_sum, backs)
    out_sum = dp_sum_second(out_sum).astype(LOW)
    query_sum = over_micro(
        [jnp.concatenate([normed[m], normed_other[m]], axis=0) for m in range(micro)], query_grad
    )
    kv_parts = jnp.stack(keyval_grad, axis=2)
    kv_swapped = swap_core(kv_parts[:, 1])
    backs[1][1] = swap_core(backs[1][1])
    query_size, query_cols = query_weight.shape
    query_sums = [
        jnp.concatenate(
            [
                query_sum[
                    i * query_size : (i + 1) * query_size, j * query_cols : (j + 1) * query_cols
                ]
                for j in range(n_line)
            ],
            axis=0,
        )
        for i in range(n_dp)
    ]
    kv_swapped, query_sums, backs, out_inward, far_out = fence(
        kv_swapped, query_sums, backs, out_inward, far_out
    )
    out_passed = [add_inward(far_out[m], out_inward[m]) for m in range(micro)]
    query_sums = dp_sum_first(query_sums)
    kv_chip = plus(kv_parts[:, 0], kv_swapped).reshape(n_line, flat, lanes)
    half = n_line // 2
    kv_near_part = kv_chip[:half].reshape(half * flat, lanes)
    kv_far_part = kv_chip[half:].reshape(half * flat, lanes)
    kv_passed = add_inward(kv_far_part, sum_inward(kv_far_part))
    kv_grad = sum_last(*sum_across(kv_near_part, kv_passed)).astype(LOW)
    kv_grad, query_sums, out_sum, out_passed = fence(kv_grad, query_sums, out_sum, out_passed)
    both = dp_sum_second(query_sums).astype(LOW)
    out_half = out_sum.shape[0] // 2
    out_crossed = [sum_across(near_out[0], out_passed[0])]
    kv_sum = contract(normed.reshape(flat, width), kv_grad, 0, 0).astype(LOW)
    kv_sum = kv_sum.reshape(n_dp, n_line, 2, kv_part, lanes)
    kv_mine = lax.dynamic_index_in_dim(kv_sum, core, 2, keepdims=False)
    kv_theirs = lax.dynamic_index_in_dim(kv_sum, 1 - core, 2, keepdims=False)
    kv_sum = plus(kv_mine, swap_core(kv_theirs))
    kv_sum = jnp.concatenate(
        [lax.dynamic_slice_in_dim(kv_sum, spot, 1, 1) for spot in order], axis=1
    ).reshape(n_dp, -1, query_cols)
    kv_sums = dp_sum_first([kv_sum[i] for i in range(n_dp)])
    both, kv_sums, kv_grad, out_passed, out_crossed, down_sum, out_sum = fence(
        both, kv_sums, kv_grad, out_passed, out_crossed, down_sum, out_sum
    )
    kv_sums = dp_sum_second(kv_sums).astype(LOW)
    out_weight_inward = sum_inward(out_sum[out_half:])
    out_crossed.append(sum_across(near_out[1], out_passed[1]))
    queries = both.reshape(n_line, query_size, query_cols)
    both = jnp.concatenate([queries, kv_sums.reshape(n_line, -1, query_cols)], axis=1)
    both_near = both[:half].reshape(-1, query_cols)
    both_far = both[half:].reshape(-1, query_cols)
    output_sums = [sum_last(*out_crossed[0])]
    both_near, both_far, kv_grad, down_sum = fence(both_near, both_far, kv_grad, down_sum)
    both_inward = sum_inward(both_far)
    down_weight_grad = dp_sum_second(down_sum)
    out_weight_sums = sum_across(
        out_sum[:out_half], add_inward(out_sum[out_half:], out_weight_inward)
    )
    input_grads = []
    gain_one_grad = shift_one_grad = query_bias_grad = 0.0
    out_bias_grad = down_bias_grad = 0.0
    for m in range(micro):
        mine, theirs = backs[m]
        grad_rows = (
            mine
            + theirs.astype(WIDE)
            + contract(kv_grad[m * rows : (m + 1) * rows], kv_full, 1, 1)
        )
        moved, gain_part, shift_part = norm_backward(tok_rows[m], gain_one, grad_rows)
        gain_one_grad = gain_one_grad + gain_part
        shift_one_grad = shift_one_grad + shift_part
        query_bias_grad = query_bias_grad + jnp.sum(query_grad[m].astype(WIDE), axis=0)
        out_bias_grad = out_bias_grad + jnp.sum(middle_low[m].astype(WIDE), axis=0)
        down_bias_grad = down_bias_grad + jnp.sum(cot_low[m].astype(WIDE), axis=0)
        input_grads.append(relative((middle_grad[m] + moved).astype(LOW), 1))
    gain_two_grad = sum(g for g, _ in norm_two_grads)
    shift_two_grad = sum(g for _, g in norm_two_grads)
    value_bias_grad = jnp.sum(kv_grad[:, HD:].astype(WIDE), axis=0)
    up_bias_grad = sum(jnp.sum(p.astype(WIDE), axis=0) for p in pre_grad)
    both_inward, both_far, out_weight_sums, out_crossed, gain_one_grad, up_bias_grad = fence(
        both_inward, both_far, out_weight_sums, out_crossed, gain_one_grad, up_bias_grad
    )
    both_crossed = sum_across(both_near, add_inward(both_far, both_inward))
    out_weight_grad = sum_last(*out_weight_sums)
    output_sums.append(sum_last(*out_crossed[1]))
    (both_crossed,) = fence(both_crossed)
    both = sum_last(*both_crossed)
    query_weight_grad = both[:query_size]
    kv_weight_grad = both[query_size:].reshape(kv_part, lanes)
    outputs = []
    for m in range(micro):
        outputs.append(relative((middle[m] + down_shift + output_sums[m]).astype(LOW), 1))

    def by_owner(vector):
        return vector.reshape(n_dp, n_mp, -1)

    query_table_grad = query_bias_grad.reshape(n_line, heads_part * HD)
    cells = query_table_grad.reshape(n_line, 1, heads_part * HD)
    spots = jnp.arange(n_line, dtype=jnp.int32)[:, None]
    query_table_grad = sum(
        jnp.where(spots == place, cells[i], 0.0) for i, place in enumerate(order)
    ).reshape(n_line, heads_part, n_dp, slim)
    query_table_grad = query_table_grad.transpose(2, 0, 1, 3)
    query_table_grad = relative(query_table_grad, 0).reshape(n_dp, n_line, 1, heads_part * slim)
    sides = jnp.arange(2, dtype=jnp.int32)[None, None, :, None]
    query_table_grad = jnp.where(sides == core, query_table_grad, 0.0)
    up_table_grad = up_bias_grad.reshape(units_part, n_dp, slim).transpose(1, 0, 2)
    up_table_grad = relative(up_table_grad, 0).reshape(n_dp, 1, units_part * slim)
    places = jnp.arange(n_mp, dtype=jnp.int32)[None, :, None]
    up_table_grad = jnp.where(places == mp, up_table_grad, 0.0)
    value_table_grad = relative(value_bias_grad.reshape(n_dp, n_mp, -1), 0)
    parts = jnp.concatenate(
        [
            by_owner(gain_one_grad),
            by_owner(shift_one_grad),
            by_owner(out_bias_grad),
            by_owner(gain_two_grad),
            by_owner(shift_two_grad),
            by_owner(down_bias_grad),
            value_table_grad,
            query_table_grad.reshape(n_dp, n_mp, -1),
            up_table_grad,
        ],
        axis=2,
    )
    mine = pack_reduce(fence(parts, both_crossed)[0])
    at = 6 * part
    value_size = value_bias.shape[0]
    query_cells = heads_part * slim
    return (
        jnp.stack(outputs),
        jnp.stack(input_grads),
        mine[:part],
        mine[part : 2 * part],
        query_weight_grad,
        mine[at + value_size : at + value_size + query_cells].reshape(heads_part, slim),
        kv_weight_grad,
        mine[at : at + value_size],
        out_weight_grad,
        mine[2 * part : 3 * part],
        mine[3 * part : 4 * part],
        mine[4 * part : 5 * part],
        up_weight_grad,
        mine[at + value_size + query_cells :].reshape(units_part, slim),
        down_weight_grad,
        mine[5 * part : 6 * part],
    )


def solution(mesh):
    both = ("dp", "mp")
    in_specs = (
        P(None, both, None),
        P(None, "dp"),
        P(None, both, None),
        P(both),
        P(both),
        P("dp", "mp"),
        P("mp", "dp"),
        P(both, None),
        P(both),
        P("mp", "dp"),
        P(both),
        P(both),
        P(both),
        P("dp", "mp"),
        P("mp", "dp"),
        P("mp", "dp"),
        P(both),
    )
    out_specs = (
        P(None, both, None),
        P(None, both, None),
        P(both),
        P(both),
        P("dp", "mp"),
        P("mp", "dp"),
        P(both, None),
        P(both),
        P("mp", "dp"),
        P(both),
        P(both),
        P(both),
        P("dp", "mp"),
        P("mp", "dp"),
        P("mp", "dp"),
        P(both),
    )
    return jax.shard_map(
        on_device, mesh=mesh, in_specs=in_specs, out_specs=out_specs, check_vma=False
    )
```

```python
import jax
import jax.numpy as jnp
from jax import lax
from jax.experimental import pallas as pl
from jax.experimental.pallas import tpu as pltpu
from jax.sharding import PartitionSpec as P

HD = 128
EPSILON = 1e-05
LOW = jnp.bfloat16
WIDE = jnp.float32


def norm_stats(rows):
    mean = jnp.mean(rows, axis=-1, keepdims=True)
    centred = rows - mean
    var = jnp.mean(centred * centred, axis=-1, keepdims=True)
    scale = lax.rsqrt(var + EPSILON)
    return centred * scale, scale


def norm_forward(rows, gain, shift):
    xhat, scale = norm_stats(rows)
    return xhat * gain + shift


def norm_backward(rows, gain, grad):
    xhat, scale = norm_stats(rows)
    scaled = grad * gain
    inner = (
        scaled
        - jnp.mean(scaled, axis=-1, keepdims=True)
        - xhat * jnp.mean(scaled * xhat, axis=-1, keepdims=True)
    )
    return scale * inner, jnp.sum(grad * xhat, axis=0), jnp.sum(grad, axis=0)


def gelu_pair(values):
    inner = 0.7978845608028654 * (values + 0.044715 * values * values * values)
    bent = jnp.tanh(inner)
    half = 0.5 * (1.0 + bent)
    slope = half + 0.5 * values * (1.0 - bent * bent) * 0.7978845608028654 * (
        1.0 + 3.0 * 0.044715 * values * values
    )
    return values * half, slope


def contract(left, right, left_dim, right_dim):
    return lax.dot_general(
        left, right, (((left_dim,), (right_dim,)), ((), ())), preferred_element_type=WIDE
    )


def swap_core(block):
    count = lax.axis_size("mp")
    return lax.ppermute(block, "mp", [(i, i ^ 1) for i in range(count)])


def shift_line(block, hops):
    count = lax.axis_size("mp")
    return lax.ppermute(block, "mp", [(i, (i + 2 * hops) % count) for i in range(count)])


def swap_dp(block, bit):
    count = lax.axis_size("dp")
    return lax.ppermute(block, "dp", [(i, i ^ bit) for i in range(count)])


def swap_mp(block, bit):
    count = lax.axis_size("mp")
    return lax.ppermute(block, "mp", [(i, i ^ bit) for i in range(count)])


def fence(*values):
    return lax.optimization_barrier(values)


def line_pairs(moves):
    return [(2 * source + side, 2 * target + side) for source, target in moves for side in (0, 1)]


def line_order():
    count = lax.axis_size("mp") // 2
    line = lax.axis_index("mp") // 2
    if count == 4:
        low_side = line < 2
        return [line, line ^ 1, jnp.where(low_side, 2, 1), jnp.where(low_side, 3, 0)]
    return [(line + count - step) % count for step in range(count)]


def line_near(block):
    count = lax.axis_size("mp") // 2
    if count == 4:
        return jnp.concatenate([block, swap_mp(block, 2)], axis=0)
    return jnp.concatenate([block] + [shift_line(block, i) for i in range(1, count // 2)], axis=0)


def line_across(block, near):
    count = lax.axis_size("mp") // 2
    if count == 4:
        return lax.ppermute(near, "mp", line_pairs([(1, 2), (2, 1)]))
    return jnp.concatenate([shift_line(block, i) for i in range(count // 2, count)], axis=0)


def line_out(across):
    if lax.axis_size("mp") // 2 == 4:
        line = lax.axis_index("mp") // 2
        outward = lax.ppermute(across, "mp", line_pairs([(1, 0), (2, 3)]))
        return jnp.where((line == 1) | (line == 2), across, outward)
    return across


def middle_swap(block):
    return lax.ppermute(block, "mp", line_pairs([(1, 2), (2, 1)]))


def move_out(block):
    return lax.ppermute(block, "mp", line_pairs([(1, 0), (2, 3)]))


def move_in(block):
    return lax.ppermute(block, "mp", line_pairs([(0, 1), (3, 2)]))


def plus(left, right):
    return (left.astype(WIDE) + right.astype(WIDE)).astype(LOW)


def four_places():
    return lax.axis_size("mp") // 2 == 4


def gather_1(own):
    if four_places():
        return swap_mp(own, 2), middle_swap(own)
    count = lax.axis_size("mp") // 2
    near = [own] + [shift_line(own, i) for i in range(1, count // 2)]
    far = [shift_line(own, i) for i in range(count // 2, count)]
    return jnp.concatenate(near, axis=0), jnp.concatenate(far, axis=0)


def gather_near(own, first):
    return jnp.concatenate([own, first[0]], axis=0) if four_places() else first[0]


def gather_2(first):
    return (middle_swap(first[0]), move_out(first[1])) if four_places() else first


def gather_3(first, second):
    if not four_places():
        return first[1]
    line = lax.axis_index("mp") // 2
    inner = (line == 1) | (line == 2)
    last = move_out(second[0])
    return jnp.concatenate(
        [jnp.where(inner, first[1], second[1]), jnp.where(inner, second[0], last)], axis=0
    )


def reduce_1(far):
    return move_in(far[far.shape[0] // 2 :]) if four_places() else far


def reduce_2(far, got):
    if not four_places():
        return got, got
    size = far.shape[0] // 2
    return middle_swap(plus(far[size:], got)), move_in(far[:size])


def reduce_3(near, far, got):
    if four_places():
        size = near.shape[0] // 2
        return (
            swap_mp(plus(near[size:], got[0]), 2),
            middle_swap(plus(far[:size], got[1])),
        )
    count = lax.axis_size("mp") // 2
    size = near.shape[0] * 2 // count
    blocks = [half[i * size : (i + 1) * size] for half in (near, far) for i in range(count // 2)]
    return [shift_line(blocks[hops], -hops) for hops in range(1, count)]


def reduce_end(near, got):
    total = near[: got[0].shape[0]].astype(WIDE)
    for part in got:
        total = total + part.astype(WIDE)
    return total


def sum_inward(far):
    return move_in(far) if four_places() else far


def add_inward(far, got):
    return plus(far, got) if four_places() else far


def sum_across(near, passed):
    if not four_places():
        return near, passed
    size = near.shape[0] // 2
    across = middle_swap(passed)
    return near[:size].astype(WIDE) + across[:size].astype(WIDE), plus(near[size:], across[size:])


def sum_last(first, second):
    if four_places():
        return first + swap_mp(second, 2).astype(WIDE)
    return reduce_end(first, reduce_3(first, second, None))


def dp_first(block):
    count = lax.axis_size("dp")
    if count == 4:
        return [block, swap_dp(block, 1), swap_dp(block, 2)]
    blocks = [block]
    bit = 1
    while bit < count:
        size = block.shape[0]
        got = swap_dp(jnp.concatenate(blocks, axis=0), bit)
        blocks = blocks + [got[i * size : (i + 1) * size] for i in range(bit)]
        bit = bit * 2
    return blocks


def dp_second(blocks):
    if lax.axis_size("dp") == 4:
        half = blocks[0].shape[0] // 2
        head, tail = swap_dp(blocks[1][:half], 2), swap_dp(blocks[2][half:], 1)
        return list(blocks) + [jnp.concatenate([head, tail], axis=0)]
    return list(blocks)


def dp_sum_first(blocks):
    if len(blocks) == 4:
        half = blocks[0].shape[0] // 2
        head = swap_dp(blocks[3][:half], 2).astype(WIDE)
        tail = swap_dp(blocks[3][half:], 1).astype(WIDE)
        one = jnp.concatenate(
            [(blocks[1][:half].astype(WIDE) + head).astype(LOW), blocks[1][half:]], axis=0
        )
        two = jnp.concatenate(
            [blocks[2][:half], (blocks[2][half:].astype(WIDE) + tail).astype(LOW)], axis=0
        )
        return [blocks[0], one, two]
    bit = len(blocks) // 2
    size = blocks[0].shape[0]
    while bit >= 1:
        got = swap_dp(jnp.concatenate(blocks[bit:], axis=0), bit).astype(WIDE)
        blocks = [
            (blocks[i].astype(WIDE) + got[i * size : (i + 1) * size]).astype(LOW)
            for i in range(bit)
        ]
        bit = bit // 2
    return blocks


def dp_sum_second(blocks):
    total = blocks[0].astype(WIDE)
    for bit, block in enumerate(blocks[1:]):
        total = total + swap_dp(block, bit + 1).astype(WIDE)
    return total


def pack_reduce(parts):
    place = lax.axis_index("mp")
    bit = parts.shape[0] // 2
    while bit >= 1:
        parts = parts[:bit] + swap_dp(parts[bit:], bit)
        bit = bit // 2
    parts = parts[0]
    bit = parts.shape[0] // 2
    while bit >= 1:
        upper = (place & bit) != 0
        low_half, high_half = parts[:bit], parts[bit:]
        sent = swap_mp(jnp.where(upper, low_half, high_half), bit)
        parts = jnp.where(upper, high_half, low_half) + sent
        bit = bit // 2
    return parts[0]


def relative(array, axis):
    count = lax.axis_size("dp")
    place = lax.axis_index("dp")
    size = array.shape[axis] // count
    return jnp.concatenate(
        [
            lax.dynamic_slice_in_dim(array, (place ^ step) * size, size, axis)
            for step in range(count)
        ],
        axis=axis,
    )


def held(array):
    zeros = (0,) * array.ndim
    return pl.BlockSpec(array.shape, lambda *_: zeros, pipeline_mode=pl.Buffered(1))


def shaped(shape, dtype=LOW):
    return jax.ShapeDtypeStruct(shape, dtype)


def attend_kernel(n, cells, *refs):
    (own, other), refs = refs[:2], refs[2:]
    weights, refs = refs[:n], refs[n:]
    shift, keyval, query_doc, query_pos, key_doc, key_pos, query, context, probs, bias = refs
    head = pl.program_id(0)
    heads, rows, _ = query.shape
    places, size = cells

    @pl.when(head == 0)
    def _():
        allowed = (query_doc[...] == key_doc[...]) & (key_pos[...] <= query_pos[...])
        bias[...] = jnp.where(allowed, 0.0, -1e30)
        chip = jnp.concatenate([own[...], other[...]], axis=0)
        cols = weights[0].shape[1]
        for place in range(places):
            total = None
            for block in range(n):
                term = contract(
                    chip[:, block * size : (block + 1) * size],
                    weights[block][place * size : (place + 1) * size, :],
                    1,
                    0,
                )
                total = term if total is None else total + term
            total = (total + shift[:, place * cols : (place + 1) * cols]).astype(LOW)
            for i in range(cols // HD):
                query[place * (cols // HD) + i] = total[:, i * HD : (i + 1) * HD]

    scores = contract(query[head], keyval[:, :HD], 1, 1) * HD ** (-0.5) + bias[...]
    weight = jnp.exp(scores - jnp.max(scores, axis=-1, keepdims=True))
    share = 1.0 / jnp.sum(weight, axis=-1, keepdims=True)
    low = (weight * share).astype(LOW)
    probs[0] = low
    context[...] = contract(low, keyval[:, HD:], 1, 0).astype(LOW)


def attend(own, other, weights, shift, keyval, query_doc, query_pos, key_doc, key_pos):
    rows, width = own.shape
    rows = 2 * rows
    keys = keyval.shape[0]
    n = len(weights)
    size = width // n
    places = weights[0].shape[0] // size
    heads = places * weights[0].shape[1] // HD
    operands = [own, other, *weights, shift[None], keyval]
    operands += [query_doc[:, None], query_pos[:, None], key_doc[None], key_pos[None]]
    return pl.pallas_call(
        lambda *refs: attend_kernel(n, (places, size), *refs),
        grid=(heads,),
        in_specs=[held(o) for o in operands],
        out_specs=[
            pl.BlockSpec((heads, rows, HD), lambda h: (0, 0, 0)),
            pl.BlockSpec((rows, HD), lambda h: (0, h)),
            pl.BlockSpec((1, rows, keys), lambda h: (h, 0, 0)),
        ],
        out_shape=[
            shaped((heads, rows, HD)),
            shaped((rows, heads * HD)),
            shaped((heads, rows, keys)),
        ],
        scratch_shapes=[pltpu.VMEM((rows, keys), WIDE)],
        compiler_params=pltpu.CompilerParams(vmem_limit_bytes=18 * 2**20),
        cost_estimate=pl.CostEstimate(
            flops=4 * rows * keys * heads * HD + 2 * rows * width * heads * HD,
            bytes_accessed=2 * heads * rows * keys + 2 * width * heads * HD,
            transcendentals=heads * rows * keys,
        ),
    )(*operands)


def project_kernel(n, *refs):
    context, weights, (own, other) = refs[0], refs[1 : 1 + n], refs[1 + n :]
    rows = own.shape[0]
    size = weights[0].shape[1]
    for block in range(n):
        cols = slice(block * size, (block + 1) * size)
        got = contract(context[...], weights[block][...], 1, 0)
        own[:, cols] = got[:rows]
        other[:, cols] = got[rows:].astype(LOW)


def project(context, weights):
    n = len(weights)
    rows, depth = context.shape
    width = n * weights[0].shape[1]
    return pl.pallas_call(
        lambda *refs: project_kernel(n, *refs),
        out_shape=[shaped((rows // 2, width), WIDE), shaped((rows // 2, width))],
        compiler_params=pltpu.CompilerParams(vmem_limit_bytes=20 * 2**20),
        cost_estimate=pl.CostEstimate(
            flops=2 * rows * depth * width, bytes_accessed=2 * depth * width, transcendentals=0
        ),
    )(context, *weights)


def attend_back_kernel(n, heads, cells, *refs):
    (own, other), refs = refs[:2], refs[2:]
    out_weights, refs = refs[:n], refs[n:]
    query_weights, refs = refs[:n], refs[n:]
    query, keyval, probs, refs = refs[0], refs[1], refs[2], refs[3:]
    query_grad, keyval_grad, back_own, back_other, context_grad, all_grad, total = refs
    head = pl.program_id(0)
    scale = HD ** (-0.5)
    places, size = cells

    @pl.when(head == 0)
    def _():
        total[...] = jnp.zeros_like(total)
        chip = jnp.concatenate([own[...], other[...]], axis=0)
        got = None
        for block in range(n):
            term = contract(chip[:, block * size : (block + 1) * size], out_weights[block][...], 1, 1)
            got = term if got is None else got + term
        got = got.astype(LOW)
        for i in range(heads):
            context_grad[i] = got[:, i * HD : (i + 1) * HD]

    low = probs[0]
    wide = low.astype(WIDE)
    given = contract(context_grad[head], keyval[:, HD:], 1, 1)
    middle = jnp.sum(wide * given, axis=-1, keepdims=True)
    score_grad = (wide * (given - middle)).astype(LOW)
    moved = (contract(score_grad, keyval[:, :HD], 1, 0) * scale).astype(LOW)
    query_grad[...] = moved
    all_grad[head] = moved
    total[:, :HD] += contract(score_grad, query[head], 0, 0)
    total[:, HD:] += contract(low, context_grad[head], 0, 0)

    @pl.when(head == heads - 1)
    def _():
        keyval_grad[:, :HD] = (total[:, :HD] * scale).astype(LOW)
        keyval_grad[:, HD:] = total[:, HD:].astype(LOW)
        cols = query_weights[0].shape[1]
        each = cols // HD
        parts = [
            jnp.concatenate([all_grad[place * each + i] for i in range(each)], axis=1)
            for place in range(places)
        ]
        rows = back_own.shape[0]
        for block in range(n):
            got = None
            for place in range(places):
                term = contract(
                    parts[place], query_weights[block][place * size : (place + 1) * size, :], 1, 1
                )
                got = term if got is None else got + term
            back_own[:, block * size : (block + 1) * size] = got[:rows]
            back_other[:, block * size : (block + 1) * size] = got[rows:].astype(LOW)


def attend_back(own, other, out_weights, query_weights, query, keyval, probs):
    rows, width = own.shape
    heads, both, _ = query.shape
    keys = keyval.shape[0]
    n = len(out_weights)
    size = width // n
    places = query_weights[0].shape[0] // size
    first = [own, other, *out_weights, *query_weights, query, keyval]
    return pl.pallas_call(
        lambda *refs: attend_back_kernel(n, heads, (places, size), *refs),
        grid=(heads,),
        in_specs=[held(o) for o in first] + [pl.BlockSpec((1, both, keys), lambda h: (h, 0, 0))],
        out_specs=[
            pl.BlockSpec((both, HD), lambda h: (0, h)),
            pl.BlockSpec((keys, 2 * HD), lambda h: (0, 0)),
            pl.BlockSpec((rows, width), lambda h: (0, 0)),
            pl.BlockSpec((rows, width), lambda h: (0, 0)),
        ],
        out_shape=[
            shaped((both, heads * HD)),
            shaped((keys, 2 * HD)),
            shaped((rows, width), WIDE),
            shaped((rows, width)),
        ],
        scratch_shapes=[
            pltpu.VMEM((heads, both, HD), LOW),
            pltpu.VMEM((heads, both, HD), LOW),
            pltpu.VMEM((keys, 2 * HD), WIDE),
        ],
        compiler_params=pltpu.CompilerParams(vmem_limit_bytes=48 * 2**20),
        cost_estimate=pl.CostEstimate(
            flops=8 * both * keys * heads * HD + 4 * both * width * heads * HD,
            bytes_accessed=2 * heads * both * keys + 4 * width * heads * HD,
            transcendentals=0,
        ),
    )(*first, probs)


def mlp_kernel(n, *refs):
    rows_in, refs = refs[:2], refs[2:]
    grads_in, refs = refs[:2], refs[2:]
    ups, refs = refs[:n], refs[n:]
    downs, refs = refs[:n], refs[n:]
    shift, hidden, pre_grad, back, out, other = refs
    size = ups[0].shape[0]
    count = rows_in[0].shape[0]
    spans = [slice(i * size, (i + 1) * size) for i in range(n)]
    for side in (1, 0):
        pre = given = None
        for block, span in enumerate(spans):
            term = contract(rows_in[side][:, span], ups[block][...], 1, 0)
            pre = term if pre is None else pre + term
        for block, span in enumerate(spans):
            term = contract(grads_in[side][:, span], downs[block][...], 1, 1)
            given = term if given is None else given + term
        value, slope = gelu_pair(pre + shift[...])
        value = value.astype(LOW)
        grad = (given * slope).astype(LOW)
        hidden[side * count : (side + 1) * count] = value
        pre_grad[side * count : (side + 1) * count] = grad
        for block, span in enumerate(spans):
            got = contract(grad, ups[block][...], 1, 1).astype(LOW)
            if side == 0:
                back[:, span] = got
            else:
                other[:count, span] = got
        for block, span in enumerate(spans):
            got = contract(value, downs[block][...], 1, 0).astype(LOW)
            if side == 0:
                out[:, span] = got
            else:
                other[count:, span] = got


def mlp(rows_in, grads_in, ups, downs, shift):
    n = len(ups)
    count, width = rows_in[0].shape
    units = ups[0].shape[1]
    return pl.pallas_call(
        lambda *refs: mlp_kernel(n, *refs),
        out_shape=[shaped((2 * count, units))] * 2
        + [shaped((count, width))] * 2
        + [shaped((2 * count, width))],
        compiler_params=pltpu.CompilerParams(vmem_limit_bytes=34 * 2**20),
        cost_estimate=pl.CostEstimate(
            flops=16 * count * units * width,
            bytes_accessed=4 * units * width + 16 * count * width,
            transcendentals=2 * count * units,
        ),
    )(*rows_in, *grads_in, *ups, *downs, shift[None])


def up_grad_kernel(n, *refs):
    lefts, rights, result = refs[:n], refs[n : -1], refs[-1]
    per = n // len(rights)
    total = None
    for i, right in enumerate(rights):
        count = right.shape[0] // per
        for j in range(per):
            term = contract(lefts[i * per + j][...], right[j * count : (j + 1) * count], 0, 0)
            total = term if total is None else total + term
    result[0] = total.astype(LOW)


def up_grad_of(lefts, rights, blocks):
    count, width = lefts[0].shape
    units = rights[0].shape[1]
    size = width // blocks
    n = len(lefts)
    return pl.pallas_call(
        lambda *refs: up_grad_kernel(n, *refs),
        grid=(blocks,),
        in_specs=[pl.BlockSpec((count, size), lambda b: (0, b))] * n + [held(r) for r in rights],
        out_specs=pl.BlockSpec((1, size, units), lambda b: (b, 0, 0)),
        out_shape=shaped((blocks, size, units)),
        compiler_params=pltpu.CompilerParams(vmem_limit_bytes=44 * 2**20),
        cost_estimate=pl.CostEstimate(
            flops=2 * n * count * width * units,
            bytes_accessed=2 * (n * count * (width + units) + width * units),
            transcendentals=0,
        ),
    )(*lefts, *rights)


def down_grad_kernel(n, *refs):
    lefts, rights, result = refs[: -n - 1], refs[-n - 1 : -1], refs[-1]
    per = n // len(lefts)
    blocks, _, size = result.shape
    for block in range(blocks):
        total = None
        for i, left in enumerate(lefts):
            count = left.shape[0] // per
            for j in range(per):
                term = contract(
                    left[j * count : (j + 1) * count],
                    rights[i * per + j][:, block * size : (block + 1) * size],
                    0,
                    0,
                )
                total = term if total is None else total + term
        result[block] = total.astype(LOW)


def down_grad_of(lefts, rights, blocks):
    count, width = rights[0].shape
    rows, units = lefts[0].shape
    n = len(rights)
    tile = min(256, units)
    return pl.pallas_call(
        lambda *refs: down_grad_kernel(n, *refs),
        grid=(units // tile,),
        in_specs=[pl.BlockSpec((rows, tile), lambda u: (0, u))] * len(lefts)
        + [held(r) for r in rights],
        out_specs=pl.BlockSpec((blocks, tile, width // blocks), lambda u: (0, u, 0)),
        out_shape=shaped((blocks, units, width // blocks)),
        compiler_params=pltpu.CompilerParams(vmem_limit_bytes=44 * 2**20),
        cost_estimate=pl.CostEstimate(
            flops=2 * n * count * width * units,
            bytes_accessed=2 * (n * count * (width + units) + width * units),
            transcendentals=0,
        ),
    )(*lefts, *rights)


def on_device(
    tokens,
    doc_ids,
    cotangent,
    norm1_gain,
    norm1_bias,
    query_weight,
    query_bias,
    kv_weight,
    value_bias,
    out_weight,
    out_bias,
    norm2_gain,
    norm2_bias,
    up_weight,
    up_bias,
    down_weight,
    down_bias,
):
    n_dp, n_mp = lax.axis_size("dp"), lax.axis_size("mp")
    n_line = n_mp // 2
    dp, mp = lax.axis_index("dp"), lax.axis_index("mp")
    line, core = mp // 2, mp % 2
    micro, rows, width = tokens.shape
    window = doc_ids.shape[1]
    part = norm1_gain.shape[0]
    kv_part = kv_weight.shape[0]
    heads_part = query_bias.shape[0]
    units_part = up_bias.shape[0]
    slim = query_bias.shape[1]

    flat = micro * rows
    lanes = 2 * HD
    order = line_order()
    tok_low = relative(tokens, 2)
    cot_low = relative(cotangent, 2)
    vectors = [norm1_gain, norm1_bias, out_bias, norm2_gain, norm2_bias, down_bias]
    vectors += [value_bias, query_bias.reshape(-1), up_bias.reshape(-1)]
    table = jnp.stack([jnp.pad(v, (0, lanes - v.shape[0])) for v in vectors])
    table = jnp.pad(table, ((0, 16 - len(vectors)), (0, 0)))
    pack = lax.all_gather(
        jnp.concatenate([kv_weight, table], axis=0), ("dp", "mp"), axis=0, tiled=True
    )

    def back_sum(got, swapped):
        return plus(got[2], swapped[: got[2].shape[0]])

    def out_sum_of(got, swapped):
        return plus(got[3], swapped[got[3].shape[0] :])

    query_near = line_near(query_weight)
    out_near = line_near(out_weight)
    up_first = dp_first(up_weight)
    query_near, out_near, cot_low, tok_low = fence(query_near, out_near, cot_low, tok_low)
    query_across = line_across(query_weight, query_near)
    cot_near = [line_near(cot_low[0])]
    query_across, out_near, cot_near, up_first = fence(query_across, out_near, cot_near, up_first)
    query_far = line_out(query_across)
    out_across = line_across(out_weight, out_near)
    up_blocks = dp_second(up_first)
    query_far, out_across, cot_near, up_blocks = fence(query_far, out_across, cot_near, up_blocks)
    query_first = dp_first(jnp.concatenate([query_near, query_far], axis=0))
    out_far = line_out(out_across)
    cot_across = [line_across(cot_low[0], cot_near[0])]
    cot_near.append(line_near(cot_low[1]))
    (pack,) = fence(pack)
    pack = pack.reshape(n_dp, n_mp, kv_part + 16, lanes)
    kv_full = relative(pack[:, :, :kv_part], 0).reshape(width, lanes)
    fixed = pack[:, :, kv_part:].astype(WIDE)
    small = relative(fixed, 0)
    gain_one, shift_one, out_shift, gain_two, shift_two, down_shift = (
        small[:, :, i, :part].reshape(width) for i in range(6)
    )
    tok_rows = [tok_low[m].astype(WIDE) for m in range(micro)]
    normed = jnp.stack([norm_forward(r, gain_one, shift_one).astype(LOW) for r in tok_rows])
    normed_other = swap_core(normed)
    query_first, out_far, normed_other, kv_full, cot_across, fixed, cot_near = fence(
        query_first, out_far, normed_other, kv_full, cot_across, fixed, cot_near
    )
    query_blocks = dp_second(query_first)
    value_shift = fixed[:, :, 6, : value_bias.shape[0]].reshape(HD)
    kv_shift = jnp.concatenate([jnp.zeros((HD,), WIDE), value_shift])
    kv_own = (contract(normed.reshape(flat, width), kv_full, 1, 0) + kv_shift).astype(LOW)
    kv_near = line_near(kv_own)
    kv_near, out_line, fixed, cot_low = fence(
        kv_near, jnp.concatenate([out_near, out_far], axis=0), fixed, cot_low
    )
    out_first = dp_first(out_line)
    kv_across = line_across(kv_own, kv_near)
    query_table = fixed[:, :, 7, : heads_part * slim].reshape(
        n_dp, n_line, 2, heads_part, slim
    )
    query_table = lax.dynamic_index_in_dim(query_table, core, 2, keepdims=False)
    query_table = query_table.transpose(1, 2, 0, 3).reshape(n_line, heads_part * HD)
    query_shift = jnp.concatenate(
        [lax.dynamic_index_in_dim(query_table, spot, 0, keepdims=False) for spot in order]
    )
    query_blocks, kv_across, query_shift = fence(query_blocks, kv_across, query_shift)
    kv_line = jnp.concatenate([kv_near, line_out(kv_across)], axis=0)
    kv_line = kv_line.reshape(n_line, flat, lanes)
    kv_stack = jnp.stack([kv_line, swap_core(kv_line)], axis=1)
    kv_stack = kv_stack.reshape(n_line, 2, micro, rows, lanes)
    keyval = [kv_stack[:, :, m].reshape(window, lanes) for m in range(micro)]
    keyval, cot_across = fence(keyval, cot_across)
    cot_far = [line_out(cot_across[0])]
    cot_across.append(line_across(cot_low[1], cot_near[1]))
    cot_own = [swap_core(cot_near[0])]
    key_starts = [(spot * 2 + side) * rows for spot in order for side in (core, 1 - core)]
    key_pos = jnp.concatenate([s + jnp.arange(rows, dtype=jnp.int32) for s in key_starts])
    query_pos = key_pos[: 2 * rows]
    context, probs, query = [], [], []
    for m in range(micro):
        key_doc = jnp.concatenate(
            [lax.dynamic_slice_in_dim(doc_ids[m], s, rows, 0) for s in key_starts]
        )
        got = attend(
            normed[m],
            normed_other[m],
            query_blocks,
            query_shift,
            keyval[m],
            key_doc[: 2 * rows],
            query_pos,
            key_doc,
            key_pos,
        )
        query.append(got[0])
        context.append(got[1])
        probs.append(got[2])
    out_first, context, cot_own, cot_far, cot_across = fence(
        out_first, context, cot_own, cot_far, cot_across
    )
    out_blocks = dp_second(out_first)
    cot_far.append(line_out(cot_across[1]))
    out_blocks, context, down_own, fixed = fence(out_blocks, context, down_weight, fixed)
    down_first = dp_first(down_own)
    middle, normed_two = [], []
    for m in range(micro):
        mine, theirs = project(context[m], out_blocks)
        middle.append(tok_rows[m] + out_shift + mine + swap_core(theirs).astype(WIDE))
        normed_two.append(norm_forward(middle[m], gain_two, shift_two).astype(LOW))
    normed_two, fixed = fence(normed_two, fixed)
    first = [gather_1(normed_two[0])]
    up_table = lax.dynamic_index_in_dim(
        fixed[:, :, 8, : units_part * slim], mp, 1, keepdims=False
    ).reshape(n_dp, units_part, slim)
    up_shift = up_table.transpose(1, 0, 2).reshape(units_part * HD)
    first, normed_two, down_first, up_shift, cot_far = fence(
        first, normed_two, down_first, up_shift, cot_far
    )
    near_rows = [gather_near(normed_two[0], first[0])]
    near_other = [swap_core(near_rows[0])]
    second = [gather_2(first[0])]
    down_blocks = dp_second(down_first)
    near_rows, near_other, second, down_blocks, cot_far, cot_near = fence(
        near_rows, near_other, second, down_blocks, cot_far, cot_near
    )

    def feed(m, half):
        rows_in = (near_rows[m], near_other[m]) if half == 0 else (far_rows[m], far_other[m])
        grads_in = (cot_near[m], cot_own[m]) if half == 0 else (cot_far[m], cot_other[m])
        return mlp(rows_in, grads_in, up_blocks, down_blocks, up_shift)

    far_rows = [gather_3(first[0], second[0])]
    cot_other = [swap_core(cot_far[0])]
    near_got = [feed(0, 0)]
    far_rows, near_got, normed_two, cot_other = fence(far_rows, near_got, normed_two, cot_other)
    first.append(gather_1(normed_two[1]))
    far_other = [swap_core(far_rows[0])]
    near_swap = [swap_core(near_got[0][4])]
    cot_own.append(swap_core(cot_near[1]))
    far_got = [feed(0, 1)]
    first, far_got, near_swap, near_got, cot_own = fence(
        first, far_got, near_swap, near_got, cot_own
    )
    second.append(gather_2(first[1]))
    far_swap = [swap_core(far_got[0][4])]
    near_rows.append(gather_near(normed_two[1], first[1]))
    near_other.append(swap_core(near_rows[1]))
    near_back = [back_sum(near_got[0], near_swap[0])]
    near_out = [out_sum_of(near_got[0], near_swap[0])]
    second, near_rows, near_other, far_swap, near_back, near_out, cot_far = fence(
        second, near_rows, near_other, far_swap, near_back, near_out, cot_far
    )
    far_back = [back_sum(far_got[0], far_swap[0])]
    far_rows.append(gather_3(first[1], second[1]))
    got_1 = [reduce_1(far_back[0])]
    cot_other.append(swap_core(cot_far[1]))
    near_got.append(feed(1, 0))
    far_rows, got_1, near_got, far_back, cot_other, far_swap = fence(
        far_rows, got_1, near_got, far_back, cot_other, far_swap
    )
    got_2 = [reduce_2(far_back[0], got_1[0])]
    far_out = [out_sum_of(far_got[0], far_swap[0])]
    far_other.append(swap_core(far_rows[1]))
    near_swap.append(swap_core(near_got[1][4]))
    far_got.append(feed(1, 1))
    got_2, near_swap, far_got, near_got, far_out = fence(
        got_2, near_swap, far_got, near_got, far_out
    )
    got_3 = [reduce_3(near_back[0], far_back[0], got_2[0])]
    far_swap.append(swap_core(far_got[1][4]))
    near_back.append(back_sum(near_got[1], near_swap[1]))
    pre_grad = [g[1] for m in range(micro) for g in (near_got[m], far_got[m])]
    row_pieces = [
        p
        for m in range(micro)
        for p in (near_rows[m], near_other[m], far_rows[m], far_other[m])
    ]
    up_grad = up_grad_of(row_pieces, pre_grad, n_dp)
    got_3, far_swap, up_grad, near_back, near_swap = fence(
        got_3, far_swap, up_grad, near_back, near_swap
    )
    far_back.append(back_sum(far_got[1], far_swap[1]))
    got_1.append(reduce_1(far_back[1]))
    up_sum = dp_sum_first([up_grad[i] for i in range(n_dp)])
    got_3, near_swap, far_swap, up_sum = fence(got_3, near_swap, far_swap, up_sum)
    near_out.append(out_sum_of(near_got[1], near_swap[1]))
    back = [reduce_end(near_back[0], got_3[0])]
    middle_grad, middle_low, middle_other = [], [], []
    norm_two_grads = []
    query_grad, keyval_grad, backs = [], [], []

    def middle_step(m):
        moved, gain_part, shift_part = norm_backward(middle[m], gain_two, back[m])
        middle_grad.append(cot_low[m].astype(WIDE) + moved)
        middle_low.append(middle_grad[m].astype(LOW))
        norm_two_grads.append((gain_part, shift_part))
        middle_other.append(swap_core(middle_low[m]))

    def attend_step(m):
        got = attend_back(
            middle_low[m], middle_other[m], out_blocks, query_blocks, query[m], keyval[m], probs[m]
        )
        query_grad.append(got[0])
        keyval_grad.append(got[1].reshape(n_line, 2, rows, lanes))
        backs.append(list(got[2:]))

    middle_step(0)
    got_1, middle_low, middle_other, far_back, far_swap, near_out, up_sum = fence(
        got_1, middle_low, middle_other, far_back, far_swap, near_out, up_sum
    )
    got_2.append(reduce_2(far_back[1], got_1[1]))
    up_weight_grad = dp_sum_second(up_sum)
    attend_step(0)
    far_out.append(out_sum_of(far_got[1], far_swap[1]))
    hidden = [g[0] for m in range(micro) for g in (near_got[m], far_got[m])]
    got_2, query_grad, hidden, far_out = fence(got_2, query_grad, hidden, far_out)
    got_3.append(reduce_3(near_back[1], far_back[1], got_2[1]))
    backs[0][1] = swap_core(backs[0][1])
    cot_pieces = [
        p for m in range(micro) for p in (cot_near[m], cot_own[m], cot_far[m], cot_other[m])
    ]
    down_grad = down_grad_of(hidden, cot_pieces, n_dp)
    got_3, down_grad, backs, up_weight_grad, far_out = fence(
        got_3, down_grad, backs, up_weight_grad, far_out
    )
    down_sum = dp_sum_first([down_grad[i] for i in range(n_dp)])
    out_inward = [sum_inward(far_out[0])]
    back.append(reduce_end(near_back[1], got_3[1]))
    middle_step(1)
    middle_low, middle_other = fence(middle_low, middle_other)

    def over_micro(left, right):
        total = contract(left[0], right[0], 0, 0)
        for m in range(1, len(left)):
            total = total + contract(left[m], right[m], 0, 0)
        return total.astype(LOW)

    out_grad = over_micro(
        context, [jnp.concatenate([middle_low[m], middle_other[m]], axis=0) for m in range(micro)]
    )
    out_grad, down_sum, far_out = fence(out_grad, down_sum, far_out)
    middle_low[1] = fence(middle_low[1], out_grad)[0]
    out_size = out_weight.shape[1]
    out_sum = dp_sum_first([out_grad[:, i * out_size : (i + 1) * out_size] for i in range(n_dp)])
    out_inward.append(sum_inward(far_out[1]))
    attend_step(1)
    query_grad, keyval_grad, out_sum, backs = fence(query_grad, keyval_grad, out_sum, backs)
    out_sum = dp_sum_second(out_sum).astype(LOW)
    query_sum = over_micro(
        [jnp.concatenate([normed[m], normed_other[m]], axis=0) for m in range(micro)], query_grad
    )
    kv_parts = jnp.stack(keyval_grad, axis=2)
    kv_swapped = swap_core(kv_parts[:, 1])
    backs[1][1] = swap_core(backs[1][1])
    query_size, query_cols = query_weight.shape
    query_sums = [
        jnp.concatenate(
            [
                query_sum[
                    i * query_size : (i + 1) * query_size, j * query_cols : (j + 1) * query_cols
                ]
                for j in range(n_line)
            ],
            axis=0,
        )
        for i in range(n_dp)
    ]
    kv_swapped, query_sums, backs, out_inward, far_out = fence(
        kv_swapped, query_sums, backs, out_inward, far_out
    )
    out_passed = [add_inward(far_out[m], out_inward[m]) for m in range(micro)]
    query_sums = dp_sum_first(query_sums)
    kv_chip = plus(kv_parts[:, 0], kv_swapped).reshape(n_line, flat, lanes)
    half = n_line // 2
    kv_near_part = kv_chip[:half].reshape(half * flat, lanes)
    kv_far_part = kv_chip[half:].reshape(half * flat, lanes)
    kv_passed = add_inward(kv_far_part, sum_inward(kv_far_part))
    kv_grad = sum_last(*sum_across(kv_near_part, kv_passed)).astype(LOW)
    kv_grad, query_sums, out_sum, out_passed = fence(kv_grad, query_sums, out_sum, out_passed)
    both = dp_sum_second(query_sums).astype(LOW)
    out_half = out_sum.shape[0] // 2
    out_crossed = [sum_across(near_out[0], out_passed[0])]
    kv_sum = contract(normed.reshape(flat, width), kv_grad, 0, 0).astype(LOW)
    kv_sum = kv_sum.reshape(n_dp, n_line, 2, kv_part, lanes)
    kv_mine = lax.dynamic_index_in_dim(kv_sum, core, 2, keepdims=False)
    kv_theirs = lax.dynamic_index_in_dim(kv_sum, 1 - core, 2, keepdims=False)
    kv_sum = plus(kv_mine, swap_core(kv_theirs))
    kv_sum = jnp.concatenate(
        [lax.dynamic_slice_in_dim(kv_sum, spot, 1, 1) for spot in order], axis=1
    ).reshape(n_dp, -1, query_cols)
    kv_sums = dp_sum_first([kv_sum[i] for i in range(n_dp)])
    both, kv_sums, kv_grad, out_passed, out_crossed, down_sum, out_sum = fence(
        both, kv_sums, kv_grad, out_passed, out_crossed, down_sum, out_sum
    )
    kv_sums = dp_sum_second(kv_sums).astype(LOW)
    out_crossed.append(sum_across(near_out[1], out_passed[1]))
    queries = both.reshape(n_line, query_size, query_cols)
    both = jnp.concatenate([queries, kv_sums.reshape(n_line, -1, query_cols)], axis=1)
    both_near = both[:half].reshape(-1, query_cols)
    both_far = both[half:].reshape(-1, query_cols)
    both_near, both_far, kv_grad, down_sum, out_sum = fence(
        both_near, both_far, kv_grad, down_sum, out_sum
    )
    both_inward = sum_inward(both_far)
    out_weight_inward = sum_inward(out_sum[out_half:])
    input_grads = []
    gain_one_grad = shift_one_grad = query_bias_grad = 0.0
    out_bias_grad = down_bias_grad = 0.0
    for m in range(micro):
        mine, theirs = backs[m]
        grad_rows = (
            mine
            + theirs.astype(WIDE)
            + contract(kv_grad[m * rows : (m + 1) * rows], kv_full, 1, 1)
        )
        moved, gain_part, shift_part = norm_backward(tok_rows[m], gain_one, grad_rows)
        gain_one_grad = gain_one_grad + gain_part
        shift_one_grad = shift_one_grad + shift_part
        query_bias_grad = query_bias_grad + jnp.sum(query_grad[m].astype(WIDE), axis=0)
        out_bias_grad = out_bias_grad + jnp.sum(middle_low[m].astype(WIDE), axis=0)
        down_bias_grad = down_bias_grad + jnp.sum(cot_low[m].astype(WIDE), axis=0)
        input_grads.append(relative((middle_grad[m] + moved).astype(LOW), 1))
    gain_two_grad = sum(g for g, _ in norm_two_grads)
    shift_two_grad = sum(g for _, g in norm_two_grads)
    value_bias_grad = jnp.sum(kv_grad[:, HD:].astype(WIDE), axis=0)
    up_bias_grad = sum(jnp.sum(p.astype(WIDE), axis=0) for p in pre_grad)
    both_inward, both_far, down_sum, gain_one_grad, up_bias_grad, out_crossed, out_sum = fence(
        both_inward, both_far, down_sum, gain_one_grad, up_bias_grad, out_crossed, out_sum
    )
    down_weight_grad = dp_sum_second(down_sum)
    both_crossed = sum_across(both_near, add_inward(both_far, both_inward))
    out_weight_sums = sum_across(
        out_sum[:out_half], add_inward(out_sum[out_half:], out_weight_inward)
    )
    both_crossed, out_crossed = fence(both_crossed, out_crossed)
    output_sums = [sum_last(*crossed) for crossed in out_crossed]
    out_weight_grad = sum_last(*out_weight_sums)
    both = sum_last(*both_crossed)
    query_weight_grad = both[:query_size]
    kv_weight_grad = both[query_size:].reshape(kv_part, lanes)
    outputs = []
    for m in range(micro):
        outputs.append(relative((middle[m] + down_shift + output_sums[m]).astype(LOW), 1))

    def by_owner(vector):
        return vector.reshape(n_dp, n_mp, -1)

    query_table_grad = query_bias_grad.reshape(n_line, heads_part * HD)
    cells = query_table_grad.reshape(n_line, 1, heads_part * HD)
    spots = jnp.arange(n_line, dtype=jnp.int32)[:, None]
    query_table_grad = sum(
        jnp.where(spots == place, cells[i], 0.0) for i, place in enumerate(order)
    ).reshape(n_line, heads_part, n_dp, slim)
    query_table_grad = query_table_grad.transpose(2, 0, 1, 3)
    query_table_grad = relative(query_table_grad, 0).reshape(n_dp, n_line, 1, heads_part * slim)
    sides = jnp.arange(2, dtype=jnp.int32)[None, None, :, None]
    query_table_grad = jnp.where(sides == core, query_table_grad, 0.0)
    up_table_grad = up_bias_grad.reshape(units_part, n_dp, slim).transpose(1, 0, 2)
    up_table_grad = relative(up_table_grad, 0).reshape(n_dp, 1, units_part * slim)
    places = jnp.arange(n_mp, dtype=jnp.int32)[None, :, None]
    up_table_grad = jnp.where(places == mp, up_table_grad, 0.0)
    value_table_grad = relative(value_bias_grad.reshape(n_dp, n_mp, -1), 0)
    parts = jnp.concatenate(
        [
            by_owner(gain_one_grad),
            by_owner(shift_one_grad),
            by_owner(out_bias_grad),
            by_owner(gain_two_grad),
            by_owner(shift_two_grad),
            by_owner(down_bias_grad),
            value_table_grad,
            query_table_grad.reshape(n_dp, n_mp, -1),
            up_table_grad,
        ],
        axis=2,
    )
    mine = pack_reduce(fence(parts, both_crossed)[0])
    at = 6 * part
    value_size = value_bias.shape[0]
    query_cells = heads_part * slim
    return (
        jnp.stack(outputs),
        jnp.stack(input_grads),
        mine[:part],
        mine[part : 2 * part],
        query_weight_grad,
        mine[at + value_size : at + value_size + query_cells].reshape(heads_part, slim),
        kv_weight_grad,
        mine[at : at + value_size],
        out_weight_grad,
        mine[2 * part : 3 * part],
        mine[3 * part : 4 * part],
        mine[4 * part : 5 * part],
        up_weight_grad,
        mine[at + value_size + query_cells :].reshape(units_part, slim),
        down_weight_grad,
        mine[5 * part : 6 * part],
    )


def solution(mesh):
    both = ("dp", "mp")
    in_specs = (
        P(None, both, None),
        P(None, "dp"),
        P(None, both, None),
        P(both),
        P(both),
        P("dp", "mp"),
        P("mp", "dp"),
        P(both, None),
        P(both),
        P("mp", "dp"),
        P(both),
        P(both),
        P(both),
        P("dp", "mp"),
        P("mp", "dp"),
        P("mp", "dp"),
        P(both),
    )
    out_specs = (
        P(None, both, None),
        P(None, both, None),
        P(both),
        P(both),
        P("dp", "mp"),
        P("mp", "dp"),
        P(both, None),
        P(both),
        P("mp", "dp"),
        P(both),
        P(both),
        P(both),
        P("dp", "mp"),
        P("mp", "dp"),
        P("mp", "dp"),
        P(both),
    )
    return jax.shard_map(
        on_device, mesh=mesh, in_specs=in_specs, out_specs=out_specs, check_vma=False
    )
```

```python
import jax
import jax.numpy as jnp
from jax import lax
from jax.experimental import pallas as pl
from jax.experimental.pallas import tpu as pltpu
from jax.sharding import PartitionSpec as P

HD = 128
EPSILON = 1e-05
LOW = jnp.bfloat16
WIDE = jnp.float32


def norm_stats(rows):
    mean = jnp.mean(rows, axis=-1, keepdims=True)
    centred = rows - mean
    var = jnp.mean(centred * centred, axis=-1, keepdims=True)
    scale = lax.rsqrt(var + EPSILON)
    return centred * scale, scale


def norm_forward(rows, gain, shift):
    xhat, scale = norm_stats(rows)
    return xhat * gain + shift


def norm_backward(rows, gain, grad):
    xhat, scale = norm_stats(rows)
    scaled = grad * gain
    inner = (
        scaled
        - jnp.mean(scaled, axis=-1, keepdims=True)
        - xhat * jnp.mean(scaled * xhat, axis=-1, keepdims=True)
    )
    return scale * inner, jnp.sum(grad * xhat, axis=0), jnp.sum(grad, axis=0)


def gelu_pair(values):
    inner = 0.7978845608028654 * (values + 0.044715 * values * values * values)
    bent = jnp.tanh(inner)
    half = 0.5 * (1.0 + bent)
    slope = half + 0.5 * values * (1.0 - bent * bent) * 0.7978845608028654 * (
        1.0 + 3.0 * 0.044715 * values * values
    )
    return values * half, slope


def contract(left, right, left_dim, right_dim):
    return lax.dot_general(
        left, right, (((left_dim,), (right_dim,)), ((), ())), preferred_element_type=WIDE
    )


def swap_core(block):
    count = lax.axis_size("mp")
    return lax.ppermute(block, "mp", [(i, i ^ 1) for i in range(count)])


def shift_line(block, hops):
    count = lax.axis_size("mp")
    return lax.ppermute(block, "mp", [(i, (i + 2 * hops) % count) for i in range(count)])


def swap_dp(block, bit):
    count = lax.axis_size("dp")
    return lax.ppermute(block, "dp", [(i, i ^ bit) for i in range(count)])


def swap_mp(block, bit):
    count = lax.axis_size("mp")
    return lax.ppermute(block, "mp", [(i, i ^ bit) for i in range(count)])


def fence(*values):
    return lax.optimization_barrier(values)


def line_pairs(moves):
    return [(2 * source + side, 2 * target + side) for source, target in moves for side in (0, 1)]


def line_order():
    count = lax.axis_size("mp") // 2
    line = lax.axis_index("mp") // 2
    if count == 4:
        low_side = line < 2
        return [line, line ^ 1, jnp.where(low_side, 2, 1), jnp.where(low_side, 3, 0)]
    return [(line + count - step) % count for step in range(count)]


def line_near(block):
    count = lax.axis_size("mp") // 2
    if count == 4:
        return jnp.concatenate([block, swap_mp(block, 2)], axis=0)
    return jnp.concatenate([block] + [shift_line(block, i) for i in range(1, count // 2)], axis=0)


def line_across(block, near):
    count = lax.axis_size("mp") // 2
    if count == 4:
        return lax.ppermute(near, "mp", line_pairs([(1, 2), (2, 1)]))
    return jnp.concatenate([shift_line(block, i) for i in range(count // 2, count)], axis=0)


def line_out(across):
    if lax.axis_size("mp") // 2 == 4:
        line = lax.axis_index("mp") // 2
        outward = lax.ppermute(across, "mp", line_pairs([(1, 0), (2, 3)]))
        return jnp.where((line == 1) | (line == 2), across, outward)
    return across


def middle_swap(block):
    return lax.ppermute(block, "mp", line_pairs([(1, 2), (2, 1)]))


def move_out(block):
    return lax.ppermute(block, "mp", line_pairs([(1, 0), (2, 3)]))


def move_in(block):
    return lax.ppermute(block, "mp", line_pairs([(0, 1), (3, 2)]))


def plus(left, right):
    return (left.astype(WIDE) + right.astype(WIDE)).astype(LOW)


def four_places():
    return lax.axis_size("mp") // 2 == 4


def gather_1(own):
    if four_places():
        return swap_mp(own, 2), middle_swap(own)
    count = lax.axis_size("mp") // 2
    near = [own] + [shift_line(own, i) for i in range(1, count // 2)]
    far = [shift_line(own, i) for i in range(count // 2, count)]
    return jnp.concatenate(near, axis=0), jnp.concatenate(far, axis=0)


def gather_near(own, first):
    return jnp.concatenate([own, first[0]], axis=0) if four_places() else first[0]


def gather_2(first):
    return (middle_swap(first[0]), move_out(first[1])) if four_places() else first


def gather_3(first, second):
    if not four_places():
        return first[1]
    line = lax.axis_index("mp") // 2
    inner = (line == 1) | (line == 2)
    last = move_out(second[0])
    return jnp.concatenate(
        [jnp.where(inner, first[1], second[1]), jnp.where(inner, second[0], last)], axis=0
    )


def reduce_1(far):
    return move_in(far[far.shape[0] // 2 :]) if four_places() else far


def reduce_2(far, got):
    if not four_places():
        return got, got
    size = far.shape[0] // 2
    return middle_swap(plus(far[size:], got)), move_in(far[:size])


def reduce_3(near, far, got):
    if four_places():
        size = near.shape[0] // 2
        return (
            swap_mp(plus(near[size:], got[0]), 2),
            middle_swap(plus(far[:size], got[1])),
        )
    count = lax.axis_size("mp") // 2
    size = near.shape[0] * 2 // count
    blocks = [half[i * size : (i + 1) * size] for half in (near, far) for i in range(count // 2)]
    return [shift_line(blocks[hops], -hops) for hops in range(1, count)]


def reduce_end(near, got):
    total = near[: got[0].shape[0]].astype(WIDE)
    for part in got:
        total = total + part.astype(WIDE)
    return total


def sum_inward(far):
    return move_in(far) if four_places() else far


def add_inward(far, got):
    return plus(far, got) if four_places() else far


def sum_across(near, passed):
    if not four_places():
        return near, passed
    size = near.shape[0] // 2
    across = middle_swap(passed)
    return near[:size].astype(WIDE) + across[:size].astype(WIDE), plus(near[size:], across[size:])


def sum_last(first, second):
    if four_places():
        return first + swap_mp(second, 2).astype(WIDE)
    return reduce_end(first, reduce_3(first, second, None))


def dp_first(block):
    count = lax.axis_size("dp")
    if count == 4:
        return [block, swap_dp(block, 1), swap_dp(block, 2)]
    blocks = [block]
    bit = 1
    while bit < count:
        size = block.shape[0]
        got = swap_dp(jnp.concatenate(blocks, axis=0), bit)
        blocks = blocks + [got[i * size : (i + 1) * size] for i in range(bit)]
        bit = bit * 2
    return blocks


def dp_second(blocks):
    if lax.axis_size("dp") == 4:
        half = blocks[0].shape[0] // 2
        head, tail = swap_dp(blocks[1][:half], 2), swap_dp(blocks[2][half:], 1)
        return list(blocks) + [jnp.concatenate([head, tail], axis=0)]
    return list(blocks)


def dp_sum_first(blocks):
    if len(blocks) == 4:
        half = blocks[0].shape[0] // 2
        head = swap_dp(blocks[3][:half], 2).astype(WIDE)
        tail = swap_dp(blocks[3][half:], 1).astype(WIDE)
        one = jnp.concatenate(
            [(blocks[1][:half].astype(WIDE) + head).astype(LOW), blocks[1][half:]], axis=0
        )
        two = jnp.concatenate(
            [blocks[2][:half], (blocks[2][half:].astype(WIDE) + tail).astype(LOW)], axis=0
        )
        return [blocks[0], one, two]
    bit = len(blocks) // 2
    size = blocks[0].shape[0]
    while bit >= 1:
        got = swap_dp(jnp.concatenate(blocks[bit:], axis=0), bit).astype(WIDE)
        blocks = [
            (blocks[i].astype(WIDE) + got[i * size : (i + 1) * size]).astype(LOW)
            for i in range(bit)
        ]
        bit = bit // 2
    return blocks


def dp_sum_second(blocks):
    total = blocks[0].astype(WIDE)
    for bit, block in enumerate(blocks[1:]):
        total = total + swap_dp(block, bit + 1).astype(WIDE)
    return total


def pack_reduce(parts):
    place = lax.axis_index("mp")
    bit = parts.shape[0] // 2
    while bit >= 1:
        parts = parts[:bit] + swap_dp(parts[bit:], bit)
        bit = bit // 2
    parts = parts[0]
    bit = parts.shape[0] // 2
    while bit >= 1:
        upper = (place & bit) != 0
        low_half, high_half = parts[:bit], parts[bit:]
        sent = swap_mp(jnp.where(upper, low_half, high_half), bit)
        parts = jnp.where(upper, high_half, low_half) + sent
        bit = bit // 2
    return parts[0]


def relative(array, axis):
    count = lax.axis_size("dp")
    place = lax.axis_index("dp")
    size = array.shape[axis] // count
    return jnp.concatenate(
        [
            lax.dynamic_slice_in_dim(array, (place ^ step) * size, size, axis)
            for step in range(count)
        ],
        axis=axis,
    )


def held(array):
    zeros = (0,) * array.ndim
    return pl.BlockSpec(array.shape, lambda *_: zeros, pipeline_mode=pl.Buffered(1))


def shaped(shape, dtype=LOW):
    return jax.ShapeDtypeStruct(shape, dtype)


def attend_kernel(n, cells, *refs):
    (own, other), refs = refs[:2], refs[2:]
    weights, refs = refs[:n], refs[n:]
    shift, keyval, query_doc, query_pos, key_doc, key_pos, query, context, probs, bias = refs
    head = pl.program_id(0)
    heads, rows, _ = query.shape
    places, size = cells

    @pl.when(head == 0)
    def _():
        allowed = (query_doc[...] == key_doc[...]) & (key_pos[...] <= query_pos[...])
        bias[...] = jnp.where(allowed, 0.0, -1e30)
        chip = jnp.concatenate([own[...], other[...]], axis=0)
        cols = weights[0].shape[1]
        for place in range(places):
            total = None
            for block in range(n):
                term = contract(
                    chip[:, block * size : (block + 1) * size],
                    weights[block][place * size : (place + 1) * size, :],
                    1,
                    0,
                )
                total = term if total is None else total + term
            total = (total + shift[:, place * cols : (place + 1) * cols]).astype(LOW)
            for i in range(cols // HD):
                query[place * (cols // HD) + i] = total[:, i * HD : (i + 1) * HD]

    scores = contract(query[head], keyval[:, :HD], 1, 1) * HD ** (-0.5) + bias[...]
    weight = jnp.exp(scores - jnp.max(scores, axis=-1, keepdims=True))
    share = 1.0 / jnp.sum(weight, axis=-1, keepdims=True)
    low = (weight * share).astype(LOW)
    probs[0] = low
    context[...] = contract(low, keyval[:, HD:], 1, 0).astype(LOW)


def attend(own, other, weights, shift, keyval, query_doc, query_pos, key_doc, key_pos):
    rows, width = own.shape
    rows = 2 * rows
    keys = keyval.shape[0]
    n = len(weights)
    size = width // n
    places = weights[0].shape[0] // size
    heads = places * weights[0].shape[1] // HD
    operands = [own, other, *weights, shift[None], keyval]
    operands += [query_doc[:, None], query_pos[:, None], key_doc[None], key_pos[None]]
    return pl.pallas_call(
        lambda *refs: attend_kernel(n, (places, size), *refs),
        grid=(heads,),
        in_specs=[held(o) for o in operands],
        out_specs=[
            pl.BlockSpec((heads, rows, HD), lambda h: (0, 0, 0)),
            pl.BlockSpec((rows, HD), lambda h: (0, h)),
            pl.BlockSpec((1, rows, keys), lambda h: (h, 0, 0)),
        ],
        out_shape=[
            shaped((heads, rows, HD)),
            shaped((rows, heads * HD)),
            shaped((heads, rows, keys)),
        ],
        scratch_shapes=[pltpu.VMEM((rows, keys), WIDE)],
        compiler_params=pltpu.CompilerParams(vmem_limit_bytes=18 * 2**20),
        cost_estimate=pl.CostEstimate(
            flops=4 * rows * keys * heads * HD + 2 * rows * width * heads * HD,
            bytes_accessed=2 * heads * rows * keys + 2 * width * heads * HD,
            transcendentals=heads * rows * keys,
        ),
    )(*operands)


def project_kernel(n, *refs):
    context, weights, (own, other) = refs[0], refs[1 : 1 + n], refs[1 + n :]
    rows = own.shape[0]
    size = weights[0].shape[1]
    for block in range(n):
        cols = slice(block * size, (block + 1) * size)
        got = contract(context[...], weights[block][...], 1, 0)
        own[:, cols] = got[:rows]
        other[:, cols] = got[rows:].astype(LOW)


def project(context, weights):
    n = len(weights)
    rows, depth = context.shape
    width = n * weights[0].shape[1]
    return pl.pallas_call(
        lambda *refs: project_kernel(n, *refs),
        out_shape=[shaped((rows // 2, width), WIDE), shaped((rows // 2, width))],
        compiler_params=pltpu.CompilerParams(vmem_limit_bytes=20 * 2**20),
        cost_estimate=pl.CostEstimate(
            flops=2 * rows * depth * width, bytes_accessed=2 * depth * width, transcendentals=0
        ),
    )(context, *weights)


def attend_back_kernel(n, heads, cells, *refs):
    (own, other), refs = refs[:2], refs[2:]
    out_weights, refs = refs[:n], refs[n:]
    query_weights, refs = refs[:n], refs[n:]
    query, keyval, probs, refs = refs[0], refs[1], refs[2], refs[3:]
    query_grad, keyval_grad, back_own, back_other, context_grad, all_grad, total = refs
    head = pl.program_id(0)
    scale = HD ** (-0.5)
    places, size = cells

    @pl.when(head == 0)
    def _():
        total[...] = jnp.zeros_like(total)
        chip = jnp.concatenate([own[...], other[...]], axis=0)
        got = None
        for block in range(n):
            term = contract(chip[:, block * size : (block + 1) * size], out_weights[block][...], 1, 1)
            got = term if got is None else got + term
        got = got.astype(LOW)
        for i in range(heads):
            context_grad[i] = got[:, i * HD : (i + 1) * HD]

    low = probs[0]
    wide = low.astype(WIDE)
    given = contract(context_grad[head], keyval[:, HD:], 1, 1)
    middle = jnp.sum(wide * given, axis=-1, keepdims=True)
    score_grad = (wide * (given - middle)).astype(LOW)
    moved = (contract(score_grad, keyval[:, :HD], 1, 0) * scale).astype(LOW)
    query_grad[...] = moved
    all_grad[head] = moved
    total[:, :HD] += contract(score_grad, query[head], 0, 0)
    total[:, HD:] += contract(low, context_grad[head], 0, 0)

    @pl.when(head == heads - 1)
    def _():
        keyval_grad[:, :HD] = (total[:, :HD] * scale).astype(LOW)
        keyval_grad[:, HD:] = total[:, HD:].astype(LOW)
        cols = query_weights[0].shape[1]
        each = cols // HD
        parts = [
            jnp.concatenate([all_grad[place * each + i] for i in range(each)], axis=1)
            for place in range(places)
        ]
        rows = back_own.shape[0]
        for block in range(n):
            got = None
            for place in range(places):
                term = contract(
                    parts[place], query_weights[block][place * size : (place + 1) * size, :], 1, 1
                )
                got = term if got is None else got + term
            back_own[:, block * size : (block + 1) * size] = got[:rows]
            back_other[:, block * size : (block + 1) * size] = got[rows:].astype(LOW)


def attend_back(own, other, out_weights, query_weights, query, keyval, probs):
    rows, width = own.shape
    heads, both, _ = query.shape
    keys = keyval.shape[0]
    n = len(out_weights)
    size = width // n
    places = query_weights[0].shape[0] // size
    first = [own, other, *out_weights, *query_weights, query, keyval]
    return pl.pallas_call(
        lambda *refs: attend_back_kernel(n, heads, (places, size), *refs),
        grid=(heads,),
        in_specs=[held(o) for o in first] + [pl.BlockSpec((1, both, keys), lambda h: (h, 0, 0))],
        out_specs=[
            pl.BlockSpec((both, HD), lambda h: (0, h)),
            pl.BlockSpec((keys, 2 * HD), lambda h: (0, 0)),
            pl.BlockSpec((rows, width), lambda h: (0, 0)),
            pl.BlockSpec((rows, width), lambda h: (0, 0)),
        ],
        out_shape=[
            shaped((both, heads * HD)),
            shaped((keys, 2 * HD)),
            shaped((rows, width), WIDE),
            shaped((rows, width)),
        ],
        scratch_shapes=[
            pltpu.VMEM((heads, both, HD), LOW),
            pltpu.VMEM((heads, both, HD), LOW),
            pltpu.VMEM((keys, 2 * HD), WIDE),
        ],
        compiler_params=pltpu.CompilerParams(vmem_limit_bytes=48 * 2**20),
        cost_estimate=pl.CostEstimate(
            flops=8 * both * keys * heads * HD + 4 * both * width * heads * HD,
            bytes_accessed=2 * heads * both * keys + 4 * width * heads * HD,
            transcendentals=0,
        ),
    )(*first, probs)


def mlp_kernel(n, *refs):
    rows_in, refs = refs[:2], refs[2:]
    grads_in, refs = refs[:2], refs[2:]
    ups, refs = refs[:n], refs[n:]
    downs, refs = refs[:n], refs[n:]
    shift, hidden, pre_grad, back, out, other = refs
    size = ups[0].shape[0]
    count = rows_in[0].shape[0]
    spans = [slice(i * size, (i + 1) * size) for i in range(n)]
    for side in (1, 0):
        pre = given = None
        for block, span in enumerate(spans):
            term = contract(rows_in[side][:, span], ups[block][...], 1, 0)
            pre = term if pre is None else pre + term
        for block, span in enumerate(spans):
            term = contract(grads_in[side][:, span], downs[block][...], 1, 1)
            given = term if given is None else given + term
        value, slope = gelu_pair(pre + shift[...])
        value = value.astype(LOW)
        grad = (given * slope).astype(LOW)
        hidden[side * count : (side + 1) * count] = value
        pre_grad[side * count : (side + 1) * count] = grad
        for block, span in enumerate(spans):
            got = contract(grad, ups[block][...], 1, 1).astype(LOW)
            if side == 0:
                back[:, span] = got
            else:
                other[:count, span] = got
        for block, span in enumerate(spans):
            got = contract(value, downs[block][...], 1, 0).astype(LOW)
            if side == 0:
                out[:, span] = got
            else:
                other[count:, span] = got


def mlp(rows_in, grads_in, ups, downs, shift):
    n = len(ups)
    count, width = rows_in[0].shape
    units = ups[0].shape[1]
    return pl.pallas_call(
        lambda *refs: mlp_kernel(n, *refs),
        out_shape=[shaped((2 * count, units))] * 2
        + [shaped((count, width))] * 2
        + [shaped((2 * count, width))],
        compiler_params=pltpu.CompilerParams(vmem_limit_bytes=34 * 2**20),
        cost_estimate=pl.CostEstimate(
            flops=16 * count * units * width,
            bytes_accessed=4 * units * width + 16 * count * width,
            transcendentals=2 * count * units,
        ),
    )(*rows_in, *grads_in, *ups, *downs, shift[None])


def up_grad_kernel(n, *refs):
    lefts, rights, result = refs[:n], refs[n : -1], refs[-1]
    per = n // len(rights)
    total = None
    for i, right in enumerate(rights):
        count = right.shape[0] // per
        for j in range(per):
            term = contract(lefts[i * per + j][...], right[j * count : (j + 1) * count], 0, 0)
            total = term if total is None else total + term
    result[0] = total.astype(LOW)


def up_grad_of(lefts, rights, blocks):
    count, width = lefts[0].shape
    units = rights[0].shape[1]
    size = width // blocks
    n = len(lefts)
    return pl.pallas_call(
        lambda *refs: up_grad_kernel(n, *refs),
        grid=(blocks,),
        in_specs=[pl.BlockSpec((count, size), lambda b: (0, b))] * n + [held(r) for r in rights],
        out_specs=pl.BlockSpec((1, size, units), lambda b: (b, 0, 0)),
        out_shape=shaped((blocks, size, units)),
        compiler_params=pltpu.CompilerParams(vmem_limit_bytes=44 * 2**20),
        cost_estimate=pl.CostEstimate(
            flops=2 * n * count * width * units,
            bytes_accessed=2 * (n * count * (width + units) + width * units),
            transcendentals=0,
        ),
    )(*lefts, *rights)


def down_grad_kernel(n, *refs):
    lefts, rights, result = refs[: -n - 1], refs[-n - 1 : -1], refs[-1]
    per = n // len(lefts)
    blocks, _, size = result.shape
    for block in range(blocks):
        total = None
        for i, left in enumerate(lefts):
            count = left.shape[0] // per
            for j in range(per):
                term = contract(
                    left[j * count : (j + 1) * count],
                    rights[i * per + j][:, block * size : (block + 1) * size],
                    0,
                    0,
                )
                total = term if total is None else total + term
        result[block] = total.astype(LOW)


def down_grad_of(lefts, rights, blocks):
    count, width = rights[0].shape
    rows, units = lefts[0].shape
    n = len(rights)
    tile = min(256, units)
    return pl.pallas_call(
        lambda *refs: down_grad_kernel(n, *refs),
        grid=(units // tile,),
        in_specs=[pl.BlockSpec((rows, tile), lambda u: (0, u))] * len(lefts)
        + [held(r) for r in rights],
        out_specs=pl.BlockSpec((blocks, tile, width // blocks), lambda u: (0, u, 0)),
        out_shape=shaped((blocks, units, width // blocks)),
        compiler_params=pltpu.CompilerParams(vmem_limit_bytes=44 * 2**20),
        cost_estimate=pl.CostEstimate(
            flops=2 * n * count * width * units,
            bytes_accessed=2 * (n * count * (width + units) + width * units),
            transcendentals=0,
        ),
    )(*lefts, *rights)


def on_device(
    tokens,
    doc_ids,
    cotangent,
    norm1_gain,
    norm1_bias,
    query_weight,
    query_bias,
    kv_weight,
    value_bias,
    out_weight,
    out_bias,
    norm2_gain,
    norm2_bias,
    up_weight,
    up_bias,
    down_weight,
    down_bias,
):
    n_dp, n_mp = lax.axis_size("dp"), lax.axis_size("mp")
    n_line = n_mp // 2
    dp, mp = lax.axis_index("dp"), lax.axis_index("mp")
    line, core = mp // 2, mp % 2
    micro, rows, width = tokens.shape
    window = doc_ids.shape[1]
    part = norm1_gain.shape[0]
    kv_part = kv_weight.shape[0]
    heads_part = query_bias.shape[0]
    units_part = up_bias.shape[0]
    slim = query_bias.shape[1]

    flat = micro * rows
    lanes = 2 * HD
    order = line_order()
    tok_low = relative(tokens, 2)
    cot_low = relative(cotangent, 2)
    vectors = [norm1_gain, norm1_bias, out_bias, norm2_gain, norm2_bias, down_bias]
    vectors += [value_bias, query_bias.reshape(-1), up_bias.reshape(-1)]
    table = jnp.stack([jnp.pad(v, (0, lanes - v.shape[0])) for v in vectors])
    table = jnp.pad(table, ((0, 16 - len(vectors)), (0, 0)))
    pack = lax.all_gather(
        jnp.concatenate([kv_weight, table], axis=0), ("dp", "mp"), axis=0, tiled=True
    )

    def back_sum(got, swapped):
        return plus(got[2], swapped[: got[2].shape[0]])

    def out_sum_of(got, swapped):
        return plus(got[3], swapped[got[3].shape[0] :])

    query_near = line_near(query_weight)
    out_near = line_near(out_weight)
    up_first = dp_first(up_weight)
    query_near, out_near, cot_low, tok_low = fence(query_near, out_near, cot_low, tok_low)
    query_across = line_across(query_weight, query_near)
    cot_near = [line_near(cot_low[0])]
    query_across, out_near, cot_near, up_first = fence(query_across, out_near, cot_near, up_first)
    query_far = line_out(query_across)
    out_across = line_across(out_weight, out_near)
    up_blocks = dp_second(up_first)
    query_far, out_across, cot_near, up_blocks = fence(query_far, out_across, cot_near, up_blocks)
    query_first = dp_first(jnp.concatenate([query_near, query_far], axis=0))
    out_far = line_out(out_across)
    cot_across = [line_across(cot_low[0], cot_near[0])]
    cot_near.append(line_near(cot_low[1]))
    (pack,) = fence(pack)
    pack = pack.reshape(n_dp, n_mp, kv_part + 16, lanes)
    kv_full = relative(pack[:, :, :kv_part], 0).reshape(width, lanes)
    fixed = pack[:, :, kv_part:].astype(WIDE)
    small = relative(fixed, 0)
    gain_one, shift_one, out_shift, gain_two, shift_two, down_shift = (
        small[:, :, i, :part].reshape(width) for i in range(6)
    )
    tok_rows = [tok_low[m].astype(WIDE) for m in range(micro)]
    normed = jnp.stack([norm_forward(r, gain_one, shift_one).astype(LOW) for r in tok_rows])
    normed_other = swap_core(normed)
    query_first, out_far, normed_other, kv_full, cot_across, fixed, cot_near = fence(
        query_first, out_far, normed_other, kv_full, cot_across, fixed, cot_near
    )
    query_blocks = dp_second(query_first)
    value_shift = fixed[:, :, 6, : value_bias.shape[0]].reshape(HD)
    kv_shift = jnp.concatenate([jnp.zeros((HD,), WIDE), value_shift])
    kv_own = (contract(normed.reshape(flat, width), kv_full, 1, 0) + kv_shift).astype(LOW)
    kv_near = line_near(kv_own)
    kv_near, out_line, fixed, cot_low = fence(
        kv_near, jnp.concatenate([out_near, out_far], axis=0), fixed, cot_low
    )
    out_first = dp_first(out_line)
    kv_across = line_across(kv_own, kv_near)
    query_table = fixed[:, :, 7, : heads_part * slim].reshape(
        n_dp, n_line, 2, heads_part, slim
    )
    query_table = lax.dynamic_index_in_dim(query_table, core, 2, keepdims=False)
    query_table = query_table.transpose(1, 2, 0, 3).reshape(n_line, heads_part * HD)
    query_shift = jnp.concatenate(
        [lax.dynamic_index_in_dim(query_table, spot, 0, keepdims=False) for spot in order]
    )
    query_blocks, kv_across, query_shift = fence(query_blocks, kv_across, query_shift)
    kv_line = jnp.concatenate([kv_near, line_out(kv_across)], axis=0)
    kv_line = kv_line.reshape(n_line, flat, lanes)
    kv_stack = jnp.stack([kv_line, swap_core(kv_line)], axis=1)
    kv_stack = kv_stack.reshape(n_line, 2, micro, rows, lanes)
    keyval = [kv_stack[:, :, m].reshape(window, lanes) for m in range(micro)]
    keyval, cot_across = fence(keyval, cot_across)
    cot_far = [line_out(cot_across[0])]
    cot_across.append(line_across(cot_low[1], cot_near[1]))
    cot_own = [swap_core(cot_near[0])]
    key_starts = [(spot * 2 + side) * rows for spot in order for side in (core, 1 - core)]
    key_pos = jnp.concatenate([s + jnp.arange(rows, dtype=jnp.int32) for s in key_starts])
    query_pos = key_pos[: 2 * rows]
    context, probs, query = [], [], []
    for m in range(micro):
        key_doc = jnp.concatenate(
            [lax.dynamic_slice_in_dim(doc_ids[m], s, rows, 0) for s in key_starts]
        )
        got = attend(
            normed[m],
            normed_other[m],
            query_blocks,
            query_shift,
            keyval[m],
            key_doc[: 2 * rows],
            query_pos,
            key_doc,
            key_pos,
        )
        query.append(got[0])
        context.append(got[1])
        probs.append(got[2])
    out_first, context, cot_own, cot_far, cot_across = fence(
        out_first, context, cot_own, cot_far, cot_across
    )
    out_blocks = dp_second(out_first)
    half_size = cot_across[1].shape[0] // 2
    cot_halves = [line_out(cot_across[1][:half_size])]
    out_blocks, context, down_own, fixed, cot_halves, cot_across = fence(
        out_blocks, context, down_weight, fixed, cot_halves, cot_across
    )
    cot_halves.append(line_out(cot_across[1][half_size:]))
    cot_far.append(jnp.concatenate(cot_halves, axis=0))
    down_first = dp_first(down_own)
    middle, normed_two = [], []
    for m in range(micro):
        mine, theirs = project(context[m], out_blocks)
        middle.append(tok_rows[m] + out_shift + mine + swap_core(theirs).astype(WIDE))
        normed_two.append(norm_forward(middle[m], gain_two, shift_two).astype(LOW))
    normed_two, fixed = fence(normed_two, fixed)
    first = [gather_1(normed_two[0])]
    up_table = lax.dynamic_index_in_dim(
        fixed[:, :, 8, : units_part * slim], mp, 1, keepdims=False
    ).reshape(n_dp, units_part, slim)
    up_shift = up_table.transpose(1, 0, 2).reshape(units_part * HD)
    first, normed_two, down_first, up_shift, cot_far = fence(
        first, normed_two, down_first, up_shift, cot_far
    )
    near_rows = [gather_near(normed_two[0], first[0])]
    near_other = [swap_core(near_rows[0])]
    second = [gather_2(first[0])]
    down_blocks = dp_second(down_first)
    near_rows, near_other, second, down_blocks, cot_far, cot_near = fence(
        near_rows, near_other, second, down_blocks, cot_far, cot_near
    )

    def feed(m, half):
        rows_in = (near_rows[m], near_other[m]) if half == 0 else (far_rows[m], far_other[m])
        grads_in = (cot_near[m], cot_own[m]) if half == 0 else (cot_far[m], cot_other[m])
        return mlp(rows_in, grads_in, up_blocks, down_blocks, up_shift)

    far_rows = [gather_3(first[0], second[0])]
    cot_other = [swap_core(cot_far[0])]
    near_got = [feed(0, 0)]
    far_rows, near_got, normed_two, cot_other = fence(far_rows, near_got, normed_two, cot_other)
    first.append(gather_1(normed_two[1]))
    far_other = [swap_core(far_rows[0])]
    near_swap = [swap_core(near_got[0][4])]
    cot_own.append(swap_core(cot_near[1]))
    far_got = [feed(0, 1)]
    first, far_got, near_swap, near_got, cot_own = fence(
        first, far_got, near_swap, near_got, cot_own
    )
    second.append(gather_2(first[1]))
    far_swap = [swap_core(far_got[0][4])]
    near_rows.append(gather_near(normed_two[1], first[1]))
    near_other.append(swap_core(near_rows[1]))
    near_back = [back_sum(near_got[0], near_swap[0])]
    near_out = [out_sum_of(near_got[0], near_swap[0])]
    second, near_rows, near_other, far_swap, near_back, near_out, cot_far = fence(
        second, near_rows, near_other, far_swap, near_back, near_out, cot_far
    )
    far_back = [back_sum(far_got[0], far_swap[0])]
    far_rows.append(gather_3(first[1], second[1]))
    got_1 = [reduce_1(far_back[0])]
    cot_other.append(swap_core(cot_far[1]))
    near_got.append(feed(1, 0))
    far_rows, got_1, near_got, far_back, cot_other, far_swap = fence(
        far_rows, got_1, near_got, far_back, cot_other, far_swap
    )
    got_2 = [reduce_2(far_back[0], got_1[0])]
    far_out = [out_sum_of(far_got[0], far_swap[0])]
    far_other.append(swap_core(far_rows[1]))
    near_swap.append(swap_core(near_got[1][4]))
    far_got.append(feed(1, 1))
    got_2, near_swap, far_got, near_got, far_out = fence(
        got_2, near_swap, far_got, near_got, far_out
    )
    got_3 = [reduce_3(near_back[0], far_back[0], got_2[0])]
    far_swap.append(swap_core(far_got[1][4]))
    near_back.append(back_sum(near_got[1], near_swap[1]))
    pre_grad = [g[1] for m in range(micro) for g in (near_got[m], far_got[m])]
    row_pieces = [
        p
        for m in range(micro)
        for p in (near_rows[m], near_other[m], far_rows[m], far_other[m])
    ]
    up_grad = up_grad_of(row_pieces, pre_grad, n_dp)
    got_3, far_swap, up_grad, near_back, near_swap = fence(
        got_3, far_swap, up_grad, near_back, near_swap
    )
    far_back.append(back_sum(far_got[1], far_swap[1]))
    got_1.append(reduce_1(far_back[1]))
    up_sum = dp_sum_first([up_grad[i] for i in range(n_dp)])
    got_3, near_swap, far_swap, up_sum = fence(got_3, near_swap, far_swap, up_sum)
    near_out.append(out_sum_of(near_got[1], near_swap[1]))
    back = [reduce_end(near_back[0], got_3[0])]
    middle_grad, middle_low, middle_other = [], [], []
    norm_two_grads = []
    query_grad, keyval_grad, backs = [], [], []

    def middle_step(m):
        moved, gain_part, shift_part = norm_backward(middle[m], gain_two, back[m])
        middle_grad.append(cot_low[m].astype(WIDE) + moved)
        middle_low.append(middle_grad[m].astype(LOW))
        norm_two_grads.append((gain_part, shift_part))
        middle_other.append(swap_core(middle_low[m]))

    def attend_step(m):
        got = attend_back(
            middle_low[m], middle_other[m], out_blocks, query_blocks, query[m], keyval[m], probs[m]
        )
        query_grad.append(got[0])
        keyval_grad.append(got[1].reshape(n_line, 2, rows, lanes))
        backs.append(list(got[2:]))

    middle_step(0)
    got_1, middle_low, middle_other, far_back, far_swap, near_out, up_sum = fence(
        got_1, middle_low, middle_other, far_back, far_swap, near_out, up_sum
    )
    got_2.append(reduce_2(far_back[1], got_1[1]))
    up_weight_grad = dp_sum_second(up_sum)
    attend_step(0)
    far_out.append(out_sum_of(far_got[1], far_swap[1]))
    hidden = [g[0] for m in range(micro) for g in (near_got[m], far_got[m])]
    got_2, query_grad, hidden, far_out = fence(got_2, query_grad, hidden, far_out)
    got_3.append(reduce_3(near_back[1], far_back[1], got_2[1]))
    backs[0][1] = swap_core(backs[0][1])
    cot_pieces = [
        p for m in range(micro) for p in (cot_near[m], cot_own[m], cot_far[m], cot_other[m])
    ]
    down_grad = down_grad_of(hidden, cot_pieces, n_dp)
    got_3, down_grad, backs, up_weight_grad, far_out = fence(
        got_3, down_grad, backs, up_weight_grad, far_out
    )
    down_sum = dp_sum_first([down_grad[i] for i in range(n_dp)])
    out_inward = [sum_inward(far_out[0])]
    back.append(reduce_end(near_back[1], got_3[1]))
    middle_step(1)
    middle_low, middle_other = fence(middle_low, middle_other)

    def over_micro(left, right):
        total = contract(left[0], right[0], 0, 0)
        for m in range(1, len(left)):
            total = total + contract(left[m], right[m], 0, 0)
        return total.astype(LOW)

    out_grad = over_micro(
        context, [jnp.concatenate([middle_low[m], middle_other[m]], axis=0) for m in range(micro)]
    )
    out_grad, down_sum, far_out = fence(out_grad, down_sum, far_out)
    middle_low[1] = fence(middle_low[1], out_grad)[0]
    out_size = out_weight.shape[1]
    out_sum = dp_sum_first([out_grad[:, i * out_size : (i + 1) * out_size] for i in range(n_dp)])
    out_inward.append(sum_inward(far_out[1]))
    attend_step(1)
    query_grad, keyval_grad, out_sum, backs = fence(query_grad, keyval_grad, out_sum, backs)
    out_sum = dp_sum_second(out_sum).astype(LOW)
    query_sum = over_micro(
        [jnp.concatenate([normed[m], normed_other[m]], axis=0) for m in range(micro)], query_grad
    )
    kv_parts = jnp.stack(keyval_grad, axis=2)
    kv_swapped = swap_core(kv_parts[:, 1])
    backs[1][1] = swap_core(backs[1][1])
    query_size, query_cols = query_weight.shape
    query_sums = [
        jnp.concatenate(
            [
                query_sum[
                    i * query_size : (i + 1) * query_size, j * query_cols : (j + 1) * query_cols
                ]
                for j in range(n_line)
            ],
            axis=0,
        )
        for i in range(n_dp)
    ]
    kv_swapped, query_sums, backs, out_inward, far_out = fence(
        kv_swapped, query_sums, backs, out_inward, far_out
    )
    out_passed = [add_inward(far_out[m], out_inward[m]) for m in range(micro)]
    query_sums = dp_sum_first(query_sums)
    kv_chip = plus(kv_parts[:, 0], kv_swapped).reshape(n_line, flat, lanes)
    half = n_line // 2
    kv_near_part = kv_chip[:half].reshape(half * flat, lanes)
    kv_far_part = kv_chip[half:].reshape(half * flat, lanes)
    kv_passed = add_inward(kv_far_part, sum_inward(kv_far_part))
    kv_grad = sum_last(*sum_across(kv_near_part, kv_passed)).astype(LOW)
    kv_grad, query_sums, out_sum, out_passed = fence(kv_grad, query_sums, out_sum, out_passed)
    both = dp_sum_second(query_sums).astype(LOW)
    out_half = out_sum.shape[0] // 2
    out_crossed = [sum_across(near_out[0], out_passed[0])]
    kv_sum = contract(normed.reshape(flat, width), kv_grad, 0, 0).astype(LOW)
    kv_sum = kv_sum.reshape(n_dp, n_line, 2, kv_part, lanes)
    kv_mine = lax.dynamic_index_in_dim(kv_sum, core, 2, keepdims=False)
    kv_theirs = lax.dynamic_index_in_dim(kv_sum, 1 - core, 2, keepdims=False)
    kv_sum = plus(kv_mine, swap_core(kv_theirs))
    kv_sum = jnp.concatenate(
        [lax.dynamic_slice_in_dim(kv_sum, spot, 1, 1) for spot in order], axis=1
    ).reshape(n_dp, -1, query_cols)
    kv_sums = dp_sum_first([kv_sum[i] for i in range(n_dp)])
    both, kv_sums, kv_grad, out_passed, out_crossed, down_sum, out_sum = fence(
        both, kv_sums, kv_grad, out_passed, out_crossed, down_sum, out_sum
    )
    kv_sums = dp_sum_second(kv_sums).astype(LOW)
    out_weight_inward = sum_inward(out_sum[out_half:])
    out_crossed.append(sum_across(near_out[1], out_passed[1]))
    queries = both.reshape(n_line, query_size, query_cols)
    both = jnp.concatenate([queries, kv_sums.reshape(n_line, -1, query_cols)], axis=1)
    both_near = both[:half].reshape(-1, query_cols)
    both_far = both[half:].reshape(-1, query_cols)
    output_sums = [sum_last(*out_crossed[0])]
    both_near, both_far, kv_grad, down_sum = fence(both_near, both_far, kv_grad, down_sum)
    both_inward = sum_inward(both_far)
    down_weight_grad = dp_sum_second(down_sum)
    out_weight_sums = sum_across(
        out_sum[:out_half], add_inward(out_sum[out_half:], out_weight_inward)
    )
    input_grads = []
    gain_one_grad = shift_one_grad = query_bias_grad = 0.0
    out_bias_grad = down_bias_grad = 0.0
    for m in range(micro):
        mine, theirs = backs[m]
        grad_rows = (
            mine
            + theirs.astype(WIDE)
            + contract(kv_grad[m * rows : (m + 1) * rows], kv_full, 1, 1)
        )
        moved, gain_part, shift_part = norm_backward(tok_rows[m], gain_one, grad_rows)
        gain_one_grad = gain_one_grad + gain_part
        shift_one_grad = shift_one_grad + shift_part
        query_bias_grad = query_bias_grad + jnp.sum(query_grad[m].astype(WIDE), axis=0)
        out_bias_grad = out_bias_grad + jnp.sum(middle_low[m].astype(WIDE), axis=0)
        down_bias_grad = down_bias_grad + jnp.sum(cot_low[m].astype(WIDE), axis=0)
        input_grads.append(relative((middle_grad[m] + moved).astype(LOW), 1))
    gain_two_grad = sum(g for g, _ in norm_two_grads)
    shift_two_grad = sum(g for _, g in norm_two_grads)
    value_bias_grad = jnp.sum(kv_grad[:, HD:].astype(WIDE), axis=0)
    up_bias_grad = sum(jnp.sum(p.astype(WIDE), axis=0) for p in pre_grad)
    both_inward, both_far, out_weight_sums, out_crossed, gain_one_grad, up_bias_grad = fence(
        both_inward, both_far, out_weight_sums, out_crossed, gain_one_grad, up_bias_grad
    )
    both_crossed = sum_across(both_near, add_inward(both_far, both_inward))
    out_weight_grad = sum_last(*out_weight_sums)
    output_sums.append(sum_last(*out_crossed[1]))
    (both_crossed,) = fence(both_crossed)
    both = sum_last(*both_crossed)
    query_weight_grad = both[:query_size]
    kv_weight_grad = both[query_size:].reshape(kv_part, lanes)
    outputs = []
    for m in range(micro):
        outputs.append(relative((middle[m] + down_shift + output_sums[m]).astype(LOW), 1))

    def by_owner(vector):
        return vector.reshape(n_dp, n_mp, -1)

    query_table_grad = query_bias_grad.reshape(n_line, heads_part * HD)
    cells = query_table_grad.reshape(n_line, 1, heads_part * HD)
    spots = jnp.arange(n_line, dtype=jnp.int32)[:, None]
    query_table_grad = sum(
        jnp.where(spots == place, cells[i], 0.0) for i, place in enumerate(order)
    ).reshape(n_line, heads_part, n_dp, slim)
    query_table_grad = query_table_grad.transpose(2, 0, 1, 3)
    query_table_grad = relative(query_table_grad, 0).reshape(n_dp, n_line, 1, heads_part * slim)
    sides = jnp.arange(2, dtype=jnp.int32)[None, None, :, None]
    query_table_grad = jnp.where(sides == core, query_table_grad, 0.0)
    up_table_grad = up_bias_grad.reshape(units_part, n_dp, slim).transpose(1, 0, 2)
    up_table_grad = relative(up_table_grad, 0).reshape(n_dp, 1, units_part * slim)
    places = jnp.arange(n_mp, dtype=jnp.int32)[None, :, None]
    up_table_grad = jnp.where(places == mp, up_table_grad, 0.0)
    value_table_grad = relative(value_bias_grad.reshape(n_dp, n_mp, -1), 0)
    parts = jnp.concatenate(
        [
            by_owner(gain_one_grad),
            by_owner(shift_one_grad),
            by_owner(out_bias_grad),
            by_owner(gain_two_grad),
            by_owner(shift_two_grad),
            by_owner(down_bias_grad),
            value_table_grad,
            query_table_grad.reshape(n_dp, n_mp, -1),
            up_table_grad,
        ],
        axis=2,
    )
    mine = pack_reduce(fence(parts, both_crossed)[0])
    at = 6 * part
    value_size = value_bias.shape[0]
    query_cells = heads_part * slim
    return (
        jnp.stack(outputs),
        jnp.stack(input_grads),
        mine[:part],
        mine[part : 2 * part],
        query_weight_grad,
        mine[at + value_size : at + value_size + query_cells].reshape(heads_part, slim),
        kv_weight_grad,
        mine[at : at + value_size],
        out_weight_grad,
        mine[2 * part : 3 * part],
        mine[3 * part : 4 * part],
        mine[4 * part : 5 * part],
        up_weight_grad,
        mine[at + value_size + query_cells :].reshape(units_part, slim),
        down_weight_grad,
        mine[5 * part : 6 * part],
    )


def solution(mesh):
    both = ("dp", "mp")
    in_specs = (
        P(None, both, None),
        P(None, "dp"),
        P(None, both, None),
        P(both),
        P(both),
        P("dp", "mp"),
        P("mp", "dp"),
        P(both, None),
        P(both),
        P("mp", "dp"),
        P(both),
        P(both),
        P(both),
        P("dp", "mp"),
        P("mp", "dp"),
        P("mp", "dp"),
        P(both),
    )
    out_specs = (
        P(None, both, None),
        P(None, both, None),
        P(both),
        P(both),
        P("dp", "mp"),
        P("mp", "dp"),
        P(both, None),
        P(both),
        P("mp", "dp"),
        P(both),
        P(both),
        P(both),
        P("dp", "mp"),
        P("mp", "dp"),
        P("mp", "dp"),
        P(both),
    )
    return jax.shard_map(
        on_device, mesh=mesh, in_specs=in_specs, out_specs=out_specs, check_vma=False
    )
```
